32 devices in a mesh: lon: 8 (over y, x, core), lat: 4 (over z).
Axes of the slice: x: 2, y: 2, z: 4, core: 2. Of those that a mesh axis runs over, the one named last changes fastest.
Arguments:
- control: float32 [2, 16, 256, 1024], P(None, None, 'lat', 'lon'), may hold values from -6 to 6
- land_mask: int32 [256, 1024], P('lat', 'lon'), may hold values 0 or 1
- std_dev: float32 [2, 16], replicated, may hold values from 0.3 to 3
- innovation: float32 [32, 16, 1024], P(None, 'lat', 'lon'), may hold values from -6 to 6
- inverse_var: float32 [32, 16, 1024], P(None, 'lat', 'lon'), may hold values from 0.25 to 4
- obs_row: int32 [16, 1024], P('lat', 'lon'), may hold values from 0 to 62
- obs_col: int32 [16, 1024], P('lat', 'lon'), may hold values from 0 to 126
- frac_row: float32 [16, 1024], P('lat', 'lon'), may hold values from 0 to 1
- frac_col: float32 [16, 1024], P('lat', 'lon'), may hold values from 0 to 1
- counts: int32 [16, 64], P('lat', 'lon'), may hold values from 0 to 16, as said below
Outputs:
- gradient: float32 [2, 16, 256, 1024], P(None, None, 'lat', 'lon')
The draws below stay inside these ranges and needn't reach their ends.
Inputs may be any that keep to these rules, and one draw needn't show every extreme that they name: `counts`: each tile gets at most 16 live slots from one holder; in every draw some tile gets exactly 16 from every holder. Dense tiles are drawn from the seed.
All inputs are finite; a program needn't handle non-finite values. No bound on the sum of `land_mask` on one device may be relied on, other than what follows from the above.
Results may differ from the reference program's by a relative error of at most 0.000075.
Values sent between devices are 32-bit elements; how exact they have to be, the bound alone decides.
A program may use at most 64 MiB of HBM per device.

```python
import math
import jax
import jax.numpy as jnp
from jax import lax

LEV = 16
CY = 64
CX = 128
HALF = 50
CAP = 16
NY = 256
NX = 1024
N_LON = 8
N_LAT = 4


def draw_counts(key, part):
    density = jax.random.randint(jax.random.fold_in(key, 11), (N_LAT, 1, N_LON, 1), 1, 5)
    baseline = jax.random.randint(jax.random.fold_in(key, 12), (N_LAT, N_LAT, N_LON, N_LON), CAP // 4, CAP + 1)
    filled = jnp.minimum(baseline * density // 4, CAP)
    full_lat = jax.random.randint(jax.random.fold_in(key, 13), (), 0, N_LAT)
    full_lon = jax.random.randint(jax.random.fold_in(key, 14), (), 0, N_LON)
    lat_index = jnp.arange(N_LAT).reshape(N_LAT, 1, 1, 1)
    lon_index = jnp.arange(N_LON).reshape(1, 1, N_LON, 1)
    chosen = (lat_index == full_lat) & (lon_index == full_lon)
    filled = jnp.where(chosen, CAP, filled)
    return filled.reshape(N_LAT * N_LAT, N_LON * N_LON).astype(jnp.int32)


def place_ends(values, own_key, low, top_value):
    longest = values.shape.index(max(values.shape))
    spots = []
    for shift in (0, 1):
        where = [jax.random.randint(jax.random.fold_in(own_key, axis), (), 0, length) for axis, length in enumerate(values.shape)]
        where[longest] = (where[longest] + shift) % values.shape[longest]
        spots.append(tuple(where))
    return values.at[spots[0]].set(low).at[spots[1]].set(top_value)


def block_scale(rng, extent, shards, smallest, high):
    level = 1.0
    for dim, parts in shards:
        steps = jax.random.uniform(jax.random.fold_in(jax.random.fold_in(rng, 6), dim), (parts,), jnp.float32, smallest / len(shards), high / len(shards))
        level = level * jnp.repeat(jnp.exp(steps), extent[dim] // parts).reshape((-1,) + (1,) * (len(extent) - 1 - dim))
    return level


def gaussian(key, dims, scale, reach, pieces=(), held_as=jnp.bfloat16):
    gain = block_scale(key, dims, pieces, -0.22, 0.18) if pieces else 1.0
    entries = jax.random.normal(key, dims, jnp.float32) * scale * gain
    return jnp.minimum(jnp.maximum(entries, -reach), reach).astype(held_as)


def setup_inputs(seed: int = 0) -> dict:
    streams_of = jax.random.split(jax.random.key(seed), 11)
    return {
        "control": gaussian(streams_of[0], (2, LEV, NY, NX), 1.0, 6.0, ((2, 4), (3, 8)), jnp.float32),
        "land_mask": place_ends((jax.random.randint(streams_of[1], (NY, NX), 0, 10) < 7).astype(jnp.int32), jax.random.fold_in(streams_of[1], 1), 0, 1),
        "std_dev": jnp.clip(jnp.exp(jax.random.uniform(streams_of[2], (2, LEV), jnp.float32, math.log(0.3), math.log(3.0))), 0.3, 3.0),
        "innovation": gaussian(streams_of[3], (2 * LEV, N_LAT * N_LAT, N_LON * N_LON * CAP), 1.0, 6.0, ((1, 4), (2, 8)), jnp.float32),
        "inverse_var": jnp.clip(jnp.exp(math.log(4.0) - 2.7725887 * jax.random.uniform(streams_of[4], (2 * LEV, N_LAT * N_LAT, N_LON * N_LON * CAP), jnp.float32) ** block_scale(streams_of[4], (2 * LEV, N_LAT * N_LAT, N_LON * N_LON * CAP), ((1, 4), (2, 8)), -0.2, 0.2)), 0.25, 4.0),
        "obs_row": place_ends(jax.random.randint(streams_of[5], (N_LAT * N_LAT, N_LON * N_LON * CAP), 0, CY - 1), jax.random.fold_in(streams_of[5], 1), 0, (CY - 1) - 1).astype(jnp.int32),
        "obs_col": place_ends(jax.random.randint(streams_of[6], (N_LAT * N_LAT, N_LON * N_LON * CAP), 0, CX - 1), jax.random.fold_in(streams_of[6], 1), 0, (CX - 1) - 1).astype(jnp.int32),
        "frac_row": jnp.clip(1.0 * jax.random.uniform(streams_of[7], (N_LAT * N_LAT, N_LON * N_LON * CAP), jnp.float32) ** block_scale(streams_of[7], (N_LAT * N_LAT, N_LON * N_LON * CAP), ((0, 4), (1, 8)), -0.2, 0.2), 0.0, 1.0),
        "frac_col": jnp.clip(1.0 * jax.random.uniform(streams_of[8], (N_LAT * N_LAT, N_LON * N_LON * CAP), jnp.float32) ** block_scale(streams_of[8], (N_LAT * N_LAT, N_LON * N_LON * CAP), ((0, 4), (1, 8)), -0.2, 0.2), 0.0, 1.0),
        "counts": draw_counts(jax.random.fold_in(streams_of[10], 71), 0),
    }


def filter_taps(half_width):
    offsets = jnp.arange(-half_width, half_width + 1).astype(jnp.float32)
    spread = half_width / 2.0
    profile = jnp.exp(-0.5 * (offsets / spread) * (offsets / spread))
    return profile / jnp.sqrt(jnp.sum(profile * profile))

def run_filter(extended, along_rows):
    taps_vector = filter_taps(HALF)
    if along_rows:
        kernel = taps_vector.reshape(1, 1, -1, 1)
    else:
        kernel = taps_vector.reshape(1, 1, 1, -1)
    output = lax.conv_general_dilated(extended[:, None], kernel, (1, 1), 'VALID', dimension_numbers=('NCHW', 'OIHW', 'NCHW'), precision=lax.Precision.HIGHEST)
    return output[:, 0]

def along_x(field):
    extended = jnp.concatenate([field[:, :, -HALF:], field, field[:, :, :HALF]], axis=2)
    return run_filter(extended, False)

def along_y(field):
    extended = jnp.pad(field, ((0, 0), (HALF, HALF), (0, 0)))
    return run_filter(extended, True)

def to_owner_order(values, rows_total):
    shaped = values.reshape(rows_total, N_LAT, N_LAT, N_LON, N_LON, CAP)
    return shaped.transpose(0, 2, 1, 4, 3, 5).reshape(rows_total, -1)

def reference(control, land_mask, std_dev, innovation, inverse_var, obs_row, obs_col, frac_row, frac_col, counts):
    rows_total = 2 * LEV
    fields = control.reshape(rows_total, NY, NX)
    ocean = land_mask.astype(jnp.float32)
    scales = std_dev.reshape(rows_total, 1, 1)
    increment = scales * ocean * along_y(along_x(ocean * fields))
    table = increment.reshape(rows_total, NY * NX)
    lat_start = (jnp.arange(N_LAT) * CY).astype(jnp.int32).reshape(N_LAT, 1, 1, 1, 1)
    lon_start = (jnp.arange(N_LON) * CX).astype(jnp.int32).reshape(1, 1, N_LON, 1, 1)
    grid_row = obs_row.reshape(N_LAT, N_LAT, N_LON, N_LON, CAP) + lat_start
    grid_col = obs_col.reshape(N_LAT, N_LAT, N_LON, N_LON, CAP) + lon_start
    corner = (grid_row * NX + grid_col).reshape(-1).astype(jnp.int32)
    row_part = frac_row.reshape(-1)
    col_part = frac_col.reshape(-1)
    stencil = [(1.0 - row_part) * (1.0 - col_part), (1.0 - row_part) * col_part, row_part * (1.0 - col_part), row_part * col_part]
    shifts = [0, 1, NX, NX + 1]
    columns = jnp.zeros((rows_total, corner.shape[0]), jnp.float32)
    for weight, offset in zip(stencil, shifts):
        columns = columns + weight[None, :] * jnp.take(table, corner + offset, axis=1)
    live_slots = counts.reshape(N_LAT, N_LAT, N_LON, N_LON, 1) > jnp.arange(CAP).astype(jnp.int32).reshape(1, 1, 1, 1, CAP)
    live = live_slots.reshape(-1).astype(jnp.float32)
    misfit = to_owner_order(inverse_var, rows_total) * (columns - to_owner_order(innovation, rows_total)) * live[None, :]
    index_all = jnp.concatenate([corner + offset for offset in shifts])
    values_all = jnp.concatenate([weight[None, :] * misfit for weight in stencil], axis=1)
    spread = jnp.zeros((rows_total, NY * NX), jnp.float32).at[:, index_all].add(values_all)
    weighted = spread.reshape(rows_total, NY, NX) * scales
    gradient = fields + ocean * along_x(along_y(ocean * weighted))
    return gradient.reshape(2, LEV, NY, NX)
```

```python
import functools

import jax
import jax.numpy as jnp
import numpy as np
from jax import lax
from jax.experimental import pallas as pl
from jax.experimental.pallas import tpu as pltpu
from jax.sharding import PartitionSpec as P

HALF = 50
SPREAD = HALF / 2.0
_TAPS = np.exp(-0.5 * (np.arange(-HALF, HALF + 1) / SPREAD) ** 2)
NORM = float(1.0 / np.sqrt(np.sum(_TAPS * _TAPS)))
CHUNK = 128
GROUPS = 4
PIECE = HALF // 2
VMEM_LIMIT = 56 * 1024 * 1024
VMEM = pl.BlockSpec(memory_space=pltpu.VMEM)
F32, BF16 = jnp.float32, jnp.bfloat16


def split(x):
    hi = x.astype(BF16)
    return hi, (x - hi.astype(F32)).astype(BF16)


def taps(distance):
    values = jnp.exp(distance * distance * (-0.5 / (SPREAD * SPREAD))) * NORM
    return jnp.where(jnp.abs(distance) < HALF + 0.5, values, 0.0)


def iota(shape, dim):
    return lax.broadcasted_iota(jnp.int32, shape, dim).astype(F32)


def dot(a, b):
    return jnp.dot(a, b, preferred_element_type=F32)


def roll(x, shift):
    shift = shift % x.shape[1]
    return pltpu.roll(x, shift, 1) if shift else x


def packing(rows):
    per = 128 // PIECE
    packed = -(-2 * rows // (8 * per)) * 8
    segments, at = [], 0
    while at < 2 * rows:
        half, row = at // rows, at % rows
        slot, place = at // packed, at % packed
        count = min(rows - row, packed - place)
        segments.append((half, row, count, slot, place))
        at += count
    return packed, segments


def pack(x, first):
    rows, width = x.shape
    packed, segments = packing(rows)
    lane = lax.broadcasted_iota(jnp.int32, (packed, width), 1)
    result = None
    for slot in range(segments[-1][3] + 1):
        mine = [s for s in segments if s[3] == slot]
        pieces = [
            roll(x[row : row + count], slot * PIECE - (first + half * PIECE))
            for half, row, count, _, _ in mine
        ]
        lacking = packed - sum(s[2] for s in mine)
        if lacking:
            pieces.append(x[:lacking])
        piece = jnp.concatenate(pieces, axis=0) if len(pieces) > 1 else pieces[0]
        result = piece if result is None else jnp.where(lane >= slot * PIECE, piece, result)
    return result


def unpack(left, right, rows):
    _, segments = packing(rows)
    lane = lax.broadcasted_iota(jnp.int32, (rows, left.shape[1]), 1)
    result = None
    for k, source in enumerate((left, right)):
        for half in range(2):
            target = k * HALF + half * PIECE
            pieces = [
                roll(source[place : place + count], target - slot * PIECE)
                for h, _, count, slot, place in segments
                if h == half
            ]
            piece = jnp.concatenate(pieces, axis=0)
            result = piece if result is None else jnp.where(lane >= target, piece, result)
    return result


def swap_blocks(blocks):
    count = len(blocks)
    width = blocks[0].shape[1] // count
    group = lax.broadcasted_iota(jnp.int32, blocks[0].shape, 1) // width
    bit = 1
    while bit < count:
        low = (group & bit) == 0
        fresh = []
        for k in range(count):
            other = blocks[k ^ bit]
            if k & bit == 0:
                fresh.append(jnp.where(low, blocks[k], roll(other, width * bit)))
            else:
                fresh.append(jnp.where(low, roll(other, -width * bit), blocks[k]))
        blocks = fresh
        bit *= 2
    return blocks


def describe(mask_ref, row_ref, col_ref, frow_ref, fcol_ref, counts_ref, out_ref):
    mask = mask_ref[...].astype(BF16)
    height, width = mask.shape
    holders, lanes = row_ref.shape
    tiles = counts_ref.shape[1]
    cap = lanes // tiles
    tile = lax.broadcasted_iota(jnp.int32, (tiles, lanes), 0)
    lane = lax.broadcasted_iota(jnp.int32, (tiles, lanes), 1)
    inside = (lane >= tile * cap) & (lane < tile * cap + cap)
    repeat = jnp.where(inside, 1.0, 0.0).astype(BF16)
    first = jnp.sum(jnp.where(inside, tile * cap, 0).astype(F32), axis=0, keepdims=True)
    number = iota((1, lanes), 1) - first
    limits = dot(counts_ref[...].astype(F32).astype(BF16), repeat)
    for s in range(holders):
        row = row_ref[pl.ds(s, 1), :].astype(F32)
        col = col_ref[pl.ds(s, 1), :].astype(F32)
        a = frow_ref[pl.ds(s, 1), :]
        b = fcol_ref[pl.ds(s, 1), :]
        x = iota((width, lanes), 0) - col
        both = jnp.concatenate(
            [jnp.where(x == 0.0, 1.0, 0.0).astype(BF16), jnp.where(x == 1.0, 1.0, 0.0).astype(BF16)], axis=1
        )
        found = dot(mask, both)
        left, right = found[:, :lanes], found[:, lanes:]
        y = iota((height, lanes), 0) - row
        m00 = jnp.sum(jnp.where(y == 0.0, left, 0.0), axis=0, keepdims=True)
        m01 = jnp.sum(jnp.where(y == 0.0, right, 0.0), axis=0, keepdims=True)
        m10 = jnp.sum(jnp.where(y == 1.0, left, 0.0), axis=0, keepdims=True)
        m11 = jnp.sum(jnp.where(y == 1.0, right, 0.0), axis=0, keepdims=True)
        live = jnp.where(number < limits[s : s + 1], 1.0, 0.0)
        at = pl.ds(s * lanes, lanes)
        out_ref[0:1, at] = row
        out_ref[1:2, at] = col
        out_ref[2:3, at] = (1.0 - a) * (1.0 - b) * m00 * live
        out_ref[3:4, at] = (1.0 - a) * b * m01 * live
        out_ref[4:5, at] = a * (1.0 - b) * m10 * live
        out_ref[5:6, at] = a * b * m11 * live
        out_ref[6:7, at] = live
        out_ref[7:8, at] = live


def kernel(
    n_lon, n_lat,
    control_ref, mask_ref, std_ref, innov_ref, ivar_ref, row_ref, col_ref, frow_ref, fcol_ref, counts_ref,
    out_ref,
    filt, halo_out, halo_in, back_out, back_in, ahl, grown, field,
    meta, onehot, weight, ytap, ylast, spreadw,
    parts, parts_in, v,
    stage, land_a, turned, land_b, owned,
    halo_ss, halo_rs, back_ss, back_rs, meta_ss, meta_rs, part_ss, part_rs, v_ss, v_rs,
    a_ss, a_rs, b_ss, b_rs,
):
    levels, height, width = control_ref.shape
    slots = meta.shape[2]
    chunks, pairs = slots // CHUNK, slots // (2 * CHUNK)
    size = levels // GROUPS
    rows = size * height
    lon, lat = lax.axis_index("lon"), lax.axis_index("lat")
    sides = [{"lon": lax.rem(lon + n_lon - 1, n_lon), "lat": lat}, {"lon": lax.rem(lon + 1, n_lon), "lat": lat}]
    ends = [({"lon": lon, "lat": lat - 1}, lat > 0), ({"lon": lon, "lat": lat + 1}, lat < n_lat - 1)]

    barrier = pltpu.get_barrier_semaphore()

    @pl.loop(1, n_lon)
    def _(d):
        pl.semaphore_signal(barrier, inc=1, device_id={"lon": lax.rem(lon + d, n_lon), "lat": lat})

    @pl.loop(1, n_lat)
    def _(d):
        pl.semaphore_signal(barrier, inc=1, device_id={"lon": lon, "lat": lax.rem(lat + d, n_lat)})

    mask = mask_ref[...].astype(F32)

    def masked(g):
        part = control_ref[g * size : (g + 1) * size] * mask[None]
        return part.reshape(rows, width)

    def side_copy(out, landed, ss, rs, g, d):
        return pltpu.make_async_remote_copy(
            src_ref=out.at[d, g], dst_ref=landed.at[1 - d, g],
            send_sem=ss.at[d, g], recv_sem=rs.at[1 - d, g], device_id=sides[d],
        )

    def side_wait(out, landed, ss, rs, g):
        for d in range(2):
            pltpu.make_async_remote_copy(
                src_ref=out.at[d, g], dst_ref=landed.at[d, g],
                send_sem=ss.at[d, g], recv_sem=rs.at[d, g], device_id=sides[d],
            ).wait_recv()

    def pack_sides(x, out, g):
        out[0, g] = pack(x, 0)
        out[1, g] = pack(x, width - HALF)

    def halo_pack(g):
        pack_sides(masked(g), halo_out, g)

    def halo_send(g):
        for d in range(2):
            side_copy(halo_out, halo_in, halo_ss, halo_rs, g, d).start()

    halo_pack(0)
    for p in range(n_lat):
        stage[p, 0:levels] = innov_ref[:, p, :]
        stage[p, levels : 2 * levels] = ivar_ref[:, p, :]
    pl.semaphore_wait(barrier, n_lon - 1 + n_lat - 1)
    halo_send(0)

    def first_copy(d):
        return pltpu.make_async_remote_copy(
            src_ref=stage.at[lax.rem(lat + d, n_lat)], dst_ref=land_a.at[lat],
            send_sem=a_ss.at[d], recv_sem=a_rs.at[d],
            device_id={"lon": lon, "lat": lax.rem(lat + d, n_lat)},
        )

    def first_wait(d):
        source = lax.rem(lat + n_lat - d, n_lat)
        pltpu.make_async_remote_copy(
            src_ref=stage.at[source], dst_ref=land_a.at[source],
            send_sem=a_ss.at[d], recv_sem=a_rs.at[d],
            device_id={"lon": lon, "lat": source},
        ).wait_recv()

    @pl.loop(1, n_lat)
    def _(d):
        first_copy(d).start()

    land_a[pl.ds(lat, 1)] = stage[pl.ds(lat, 1)]

    describe(mask_ref, row_ref, col_ref, frow_ref, fcol_ref, counts_ref, meta.at[1])

    def end_copy(src, dst, send_sem, recv_sem, d):
        return pltpu.make_async_remote_copy(
            src_ref=src, dst_ref=dst, send_sem=send_sem, recv_sem=recv_sem, device_id=ends[d][0]
        )

    def at_ends(body):
        for d in range(2):
            pl.when(ends[d][1])(functools.partial(body, d))

    def meta_copy(d):
        return end_copy(meta.at[1], meta.at[2 * (1 - d)], meta_ss.at[d], meta_rs.at[1 - d], d)

    at_ends(lambda d: meta_copy(d).start())
    for g in range(1, GROUPS):
        halo_pack(g)
        halo_send(g)

    for d in range(2):

        @pl.when(jnp.logical_not(ends[d][1]))
        def _():
            meta[2 * d] = jnp.zeros(meta.shape[1:], F32)
            v[2 * d] = jnp.zeros(v.shape[1:], F32)
            parts_in[d] = jnp.zeros(parts_in.shape[1:], F32)

    k = iota((2 * width, width), 0)
    place = jnp.where(k < width, k, jnp.where(k < width + HALF, k - (width + HALF), k - HALF))
    place = jnp.where(k < width + 2 * HALF, place, 1000.0)
    ghi, glo = split(taps(place - iota((2 * width, width), 1)))
    filt[:, 0:width] = ghi
    filt[:, width : 2 * width] = glo

    def tables(t):
        shift = float((t - 1) * height)

        @pl.loop(0, chunks)
        def _(c):
            at = pl.ds(pl.multiple_of(c * CHUNK, CHUNK), CHUNK)
            m = meta[t, :, at]
            y = m[0:1] + shift - iota((height, CHUNK), 0)
            near, far = taps(y), taps(y + 1.0)
            weight[t, c, :, 0:CHUNK] = m[2:3] * near + m[4:5] * far
            weight[t, c, :, CHUNK : 2 * CHUNK] = m[3:4] * near + m[5:6] * far
            ytap[t, :, at] = near
            ylast[t, :, at] = taps(m[0:1] + (shift + 1.0) + 0.0 * iota((8, CHUNK), 0))
            x = iota((width, CHUNK), 0) - m[1:2]
            onehot[t, c, :, 0:CHUNK] = jnp.where(x == 0.0, 1.0, 0.0).astype(BF16)
            onehot[t, c, :, CHUNK : 2 * CHUNK] = jnp.where(x == 1.0, 1.0, 0.0).astype(BF16)
            turn = jnp.transpose(m)
            x = iota((CHUNK, width), 1) - turn[:, 1:2]
            w = jnp.concatenate(
                [
                    jnp.where(x == 0.0, turn[:, 2 + 2 * i : 3 + 2 * i], 0.0)
                    + jnp.where(x == 1.0, turn[:, 3 + 2 * i : 4 + 2 * i], 0.0)
                    for i in range(2)
                ],
                axis=1,
            )
            hi, lo = split(w)
            spreadw[t, 0, at, :] = hi
            spreadw[t, 1, at, :] = lo

    tables(1)

    @pl.loop(1, n_lat)
    def _(d):
        first_wait(d)

    deep = 2 * levels // n_lon
    blocks = [land_a[:, i * deep : (i + 1) * deep, :].reshape(n_lat * deep, width) for i in range(n_lon)]
    for q, block in enumerate(swap_blocks(blocks)):
        turned[q] = block

    def second_copy(d):
        return pltpu.make_async_remote_copy(
            src_ref=turned.at[lax.rem(lon + d, n_lon)], dst_ref=land_b.at[lon],
            send_sem=b_ss.at[d], recv_sem=b_rs.at[d],
            device_id={"lon": lax.rem(lon + d, n_lon), "lat": lat},
        )

    def second_wait(d):
        source = lax.rem(lon + n_lon - d, n_lon)
        pltpu.make_async_remote_copy(
            src_ref=turned.at[source], dst_ref=land_b.at[source],
            send_sem=b_ss.at[d], recv_sem=b_rs.at[d],
            device_id={"lon": source, "lat": lat},
        ).wait_recv()

    @pl.loop(1, n_lon)
    def _(d):
        second_copy(d).start()

    land_b[pl.ds(lon, 1)] = turned[pl.ds(lon, 1)]

    for d in range(2):

        @pl.when(ends[d][1])
        def _(d=d):
            end_copy(meta.at[1], meta.at[2 * d], meta_ss.at[d], meta_rs.at[d], d).wait_recv()

        tables(2 * d)

    def take_observations():
        @pl.loop(1, n_lon)
        def _(d):
            second_wait(d)

        for i, block in enumerate(swap_blocks([land_b[t] for t in range(n_lon)])):
            for s in range(n_lat):
                owned[i * deep : (i + 1) * deep, s * width : (s + 1) * width] = block[s * deep : (s + 1) * deep]

    def smooth(x, beyond):
        hi, lo = split(jnp.concatenate([x, beyond], axis=1))
        wide = dot(hi, filt[...])
        return wide[:, :width] + wide[:, width:] + dot(lo, filt[:, 0:width])

    def part_copy(g, d):
        return end_copy(parts.at[2 * d, g], parts_in.at[1 - d, g], part_ss.at[d, g], part_rs.at[1 - d, g], d)

    def forward(g):
        side_wait(halo_out, halo_in, halo_ss, halo_rs, g)
        hi, lo = split(smooth(masked(g), unpack(halo_in[0, g], halo_in[1, g], rows)))
        ahl[:, 0:width] = hi
        ahl[:, width : 2 * width] = lo
        for t in (0, 2, 1):

            @pl.loop(0, chunks)
            def _(c):
                one = onehot[t, c]
                wide = dot(ahl[...], jnp.concatenate([one, one], axis=0))
                total = jnp.sum(wide.reshape(size, height, 2 * CHUNK) * weight[t, c][None], axis=1)
                at = pl.ds(pl.multiple_of(c * CHUNK, CHUNK), CHUNK)
                parts[t, g, :, at] = total[:, :CHUNK] + total[:, CHUNK:]

            if t == 2:
                at_ends(lambda d: part_copy(g, d).start())

    def v_copy(g, d):
        return end_copy(v.at[1, g], v.at[2 * (1 - d), g], v_ss.at[d, g], v_rs.at[1 - d, g], d)

    def misfit(g):
        at_ends(
            lambda d: end_copy(
                parts.at[2 * d, g], parts_in.at[d, g], part_ss.at[d, g], part_rs.at[d, g], d
            ).wait_recv()
        )
        scale = std_ref[g * size : (g + 1) * size, :]
        total = parts[1, g] + parts_in[0, g] + parts_in[1, g]
        first = g * size
        innov = owned[first : first + size, :]
        ivar = owned[levels + first : levels + first + size, :]
        v[1, g] = scale * ivar * (scale * total - innov)
        at_ends(lambda d: v_copy(g, d).start())

    def backward(g):
        def add(t, start):
            @pl.loop(0, pairs)
            def _(c):
                at = pl.ds(pl.multiple_of(c * 2 * CHUNK, 2 * CHUNK), 2 * CHUNK)
                value = v[t, g, :, at]
                b = (value[:, None, :] * ytap[t, :, at][None]).reshape(rows, 2 * CHUNK)
                last = value * ylast[t, 0:1, at]
                extra = jnp.concatenate([last, jnp.zeros((grown.shape[0] - rows - size, 2 * CHUNK), F32)], axis=0)
                hi, lo = split(jnp.concatenate([b, extra], axis=0))
                whi, wlo = spreadw[t, 0, at, :], spreadw[t, 1, at, :]
                total = dot(jnp.concatenate([hi, lo, hi], axis=1), jnp.concatenate([whi, whi, wlo], axis=0))
                grown[...] += total

        grown[...] = jnp.zeros_like(grown)
        add(1, True)
        for d in range(2):

            @pl.when(ends[d][1])
            def _(d=d):
                end_copy(v.at[1, g], v.at[2 * d, g], v_ss.at[d, g], v_rs.at[d, g], d).wait_recv()

            add(2 * d, False)
        below = pltpu.roll(grown[0:rows, width : 2 * width], 1, 0)
        first = grown[rows : rows + size, width : 2 * width]
        first = jnp.broadcast_to(first[:, None, :], (size, height, width)).reshape(rows, width)
        row = lax.broadcasted_iota(jnp.int32, (size, height, width), 1).reshape(rows, width)
        x = grown[0:rows, 0:width] + jnp.where(row == 0, first, below)
        field[g] = x
        pack_sides(x, back_out, g)
        for d in range(2):
            side_copy(back_out, back_in, back_ss, back_rs, g, d).start()

    def finish(g):
        side_wait(back_out, back_in, back_ss, back_rs, g)
        x = smooth(field[g], unpack(back_in[0, g], back_in[1, g], rows))
        at = slice(g * size, (g + 1) * size)
        out_ref[at] = control_ref[at] + mask[None] * x.reshape(size, height, width)

    for step in range(GROUPS + 3):
        if step < GROUPS:
            forward(step)
        if step == 1:
            take_observations()
        if 0 <= step - 1 < GROUPS:
            misfit(step - 1)
        if 0 <= step - 2 < GROUPS:
            backward(step - 2)
        if 0 <= step - 4 < GROUPS:
            finish(step - 4)
    finish(GROUPS - 1)

    for g in range(GROUPS):
        for d in range(2):
            side_copy(halo_out, halo_in, halo_ss, halo_rs, g, d).wait_send()
            side_copy(back_out, back_in, back_ss, back_rs, g, d).wait_send()
        at_ends(lambda d: part_copy(g, d).wait_send())
        at_ends(lambda d: v_copy(g, d).wait_send())
    at_ends(lambda d: meta_copy(d).wait_send())

    @pl.loop(1, n_lat)
    def _(d):
        first_copy(d).wait_send()

    @pl.loop(1, n_lon)
    def _(d):
        second_copy(d).wait_send()


def shards(n_lon, n_lat, control, land_mask, std_dev, innovation, inverse_var, *slots_of):
    levels = control.shape[0] * control.shape[1]
    height, width = control.shape[2:]
    slots = slots_of[0].shape[0] * slots_of[0].shape[1]
    chunks = slots // CHUNK
    size = levels // GROUPS
    rows = size * height
    packed = packing(rows)[0]
    grown = -(-(rows + size) // 16) * 16
    deep = 2 * levels // n_lon
    dma = pltpu.SemaphoreType.DMA
    group = dma((2, GROUPS))
    sides = pltpu.VMEM((2, GROUPS, packed, width), F32)

    gradient = pl.pallas_call(
        functools.partial(kernel, n_lon, n_lat),
        out_shape=jax.ShapeDtypeStruct((levels, height, width), F32),
        in_specs=[VMEM] * 10,
        out_specs=VMEM,
        scratch_shapes=[
            pltpu.VMEM((2 * width, 2 * width), BF16),
            sides, sides, sides, sides,
            pltpu.VMEM((rows, 2 * width), BF16),
            pltpu.VMEM((grown, 2 * width), F32),
            pltpu.VMEM((GROUPS, rows, width), F32),
            pltpu.VMEM((3, 8, slots), F32),
            pltpu.VMEM((3, chunks, width, 2 * CHUNK), BF16),
            pltpu.VMEM((3, chunks, height, 2 * CHUNK), F32),
            pltpu.VMEM((3, height, slots), F32),
            pltpu.VMEM((3, 8, slots), F32),
            pltpu.VMEM((3, 2, slots, 2 * width), BF16),
            pltpu.VMEM((3, GROUPS, size, slots), F32),
            pltpu.VMEM((2, GROUPS, size, slots), F32),
            pltpu.VMEM((3, GROUPS, size, slots), F32),
            pltpu.VMEM((n_lat, 2 * levels, width), F32),
            pltpu.VMEM((n_lat, 2 * levels, width), F32),
            pltpu.VMEM((n_lon, n_lat * deep, width), F32),
            pltpu.VMEM((n_lon, n_lat * deep, width), F32),
            pltpu.VMEM((2 * levels, slots), F32),
            group, group, group, group, dma((2,)), dma((2,)), group, group, group, group,
            dma((n_lat,)), dma((n_lat,)), dma((n_lon,)), dma((n_lon,)),
        ],
        compiler_params=pltpu.CompilerParams(
            vmem_limit_bytes=VMEM_LIMIT, collective_id=0, has_side_effects=True
        ),
        name="gradient",
    )(
        control.reshape(levels, height, width), land_mask, std_dev.reshape(levels, 1),
        innovation, inverse_var, *slots_of,
    )
    return gradient.reshape(control.shape)


def solution(mesh):
    tile = P("lat", "lon")
    in_specs = (
        P(None, None, "lat", "lon"), tile, P(),
        P(None, "lat", "lon"), P(None, "lat", "lon"),
        tile, tile, tile, tile, tile,
    )
    body = functools.partial(shards, mesh.shape["lon"], mesh.shape["lat"])
    return jax.shard_map(
        body, mesh=mesh, in_specs=in_specs,
        out_specs=P(None, None, "lat", "lon"), check_vma=False,
    )
```

```python
import functools

import jax
import jax.numpy as jnp
import numpy as np
from jax import lax
from jax.experimental import pallas as pl
from jax.experimental.pallas import tpu as pltpu
from jax.sharding import PartitionSpec as P

HALF = 50
SPREAD = HALF / 2.0
_TAPS = np.exp(-0.5 * (np.arange(-HALF, HALF + 1) / SPREAD) ** 2)
NORM = float(1.0 / np.sqrt(np.sum(_TAPS * _TAPS)))
CHUNK = 128
GROUPS = 4
PIECE = HALF // 2
VMEM = pl.BlockSpec(memory_space=pltpu.VMEM)
HBM = pl.BlockSpec(memory_space=pltpu.HBM)
F32, BF16 = jnp.float32, jnp.bfloat16


def split(x):
    hi = x.astype(BF16)
    return hi, (x - hi.astype(F32)).astype(BF16)


def taps(distance):
    values = jnp.exp(distance * distance * (-0.5 / (SPREAD * SPREAD))) * NORM
    return jnp.where(jnp.abs(distance) < HALF + 0.5, values, 0.0)


def iota(shape, dim):
    return lax.broadcasted_iota(jnp.int32, shape, dim).astype(F32)


def dot(a, b):
    return jnp.dot(a, b, preferred_element_type=F32)


def roll(x, shift):
    shift = shift % x.shape[1]
    return pltpu.roll(x, shift, 1) if shift else x


def packing(rows):
    per = 128 // PIECE
    packed = -(-2 * rows // (8 * per)) * 8
    segments, at = [], 0
    while at < 2 * rows:
        half, row = at // rows, at % rows
        slot, place = at // packed, at % packed
        count = min(rows - row, packed - place)
        segments.append((half, row, count, slot, place))
        at += count
    return packed, segments


def pack(x, first):
    rows, width = x.shape
    packed, segments = packing(rows)
    lane = lax.broadcasted_iota(jnp.int32, (packed, width), 1)
    result = None
    for slot in range(segments[-1][3] + 1):
        mine = [s for s in segments if s[3] == slot]
        pieces = [
            roll(x[row : row + count], slot * PIECE - (first + half * PIECE))
            for half, row, count, _, _ in mine
        ]
        lacking = packed - sum(s[2] for s in mine)
        if lacking:
            pieces.append(x[:lacking])
        piece = jnp.concatenate(pieces, axis=0) if len(pieces) > 1 else pieces[0]
        result = piece if result is None else jnp.where(lane >= slot * PIECE, piece, result)
    return result


def unpack(left, right, rows):
    _, segments = packing(rows)
    lane = lax.broadcasted_iota(jnp.int32, (rows, left.shape[1]), 1)
    result = None
    for k, source in enumerate((left, right)):
        for half in range(2):
            target = k * HALF + half * PIECE
            pieces = [
                roll(source[place : place + count], target - slot * PIECE)
                for h, _, count, slot, place in segments
                if h == half
            ]
            piece = jnp.concatenate(pieces, axis=0)
            result = piece if result is None else jnp.where(lane >= target, piece, result)
    return result


def swap_blocks(blocks):
    count = len(blocks)
    width = blocks[0].shape[1] // count
    group = lax.broadcasted_iota(jnp.int32, blocks[0].shape, 1) // width
    bit = 1
    while bit < count:
        low = (group & bit) == 0
        fresh = []
        for k in range(count):
            other = blocks[k ^ bit]
            if k & bit == 0:
                fresh.append(jnp.where(low, blocks[k], roll(other, width * bit)))
            else:
                fresh.append(jnp.where(low, roll(other, -width * bit), blocks[k]))
        blocks = fresh
        bit *= 2
    return blocks


def describe(mask_ref, row_ref, col_ref, frow_ref, fcol_ref, counts_ref, out_ref):
    mask = mask_ref[...].astype(BF16)
    height, width = mask.shape
    holders, lanes = row_ref.shape
    tiles = counts_ref.shape[1]
    cap = lanes // tiles
    tile = lax.broadcasted_iota(jnp.int32, (tiles, lanes), 0)
    lane = lax.broadcasted_iota(jnp.int32, (tiles, lanes), 1)
    inside = (lane >= tile * cap) & (lane < tile * cap + cap)
    repeat = jnp.where(inside, 1.0, 0.0).astype(BF16)
    first = jnp.sum(jnp.where(inside, tile * cap, 0).astype(F32), axis=0, keepdims=True)
    number = iota((1, lanes), 1) - first
    limits = dot(counts_ref[...].astype(F32).astype(BF16), repeat)
    for s in range(holders):
        row = row_ref[pl.ds(s, 1), :].astype(F32)
        col = col_ref[pl.ds(s, 1), :].astype(F32)
        a = frow_ref[pl.ds(s, 1), :]
        b = fcol_ref[pl.ds(s, 1), :]
        x = iota((width, lanes), 0) - col
        both = jnp.concatenate(
            [jnp.where(x == 0.0, 1.0, 0.0).astype(BF16), jnp.where(x == 1.0, 1.0, 0.0).astype(BF16)], axis=1
        )
        found = dot(mask, both)
        left, right = found[:, :lanes], found[:, lanes:]
        y = iota((height, lanes), 0) - row
        m00 = jnp.sum(jnp.where(y == 0.0, left, 0.0), axis=0, keepdims=True)
        m01 = jnp.sum(jnp.where(y == 0.0, right, 0.0), axis=0, keepdims=True)
        m10 = jnp.sum(jnp.where(y == 1.0, left, 0.0), axis=0, keepdims=True)
        m11 = jnp.sum(jnp.where(y == 1.0, right, 0.0), axis=0, keepdims=True)
        live = jnp.where(number < limits[s : s + 1], 1.0, 0.0)
        at = pl.ds(s * lanes, lanes)
        out_ref[0:1, at] = row
        out_ref[1:2, at] = col
        out_ref[2:3, at] = (1.0 - a) * (1.0 - b) * m00 * live
        out_ref[3:4, at] = (1.0 - a) * b * m01 * live
        out_ref[4:5, at] = a * (1.0 - b) * m10 * live
        out_ref[5:6, at] = a * b * m11 * live
        out_ref[6:7, at] = live
        out_ref[7:8, at] = live


def kernel(
    n_lon, n_lat,
    control_far, mask_far, std_far, innov_far, ivar_far, row_far, col_far, frow_far, fcol_far, counts_far,
    out_ref,
    control_ref, mask_ref, std_ref, innov_ref, ivar_ref, row_ref, col_ref, frow_ref, fcol_ref, counts_ref,
    filt, halo_out, halo_in, back_out, back_in, ahl, grown, field,
    meta, onehot, weight, ytap, ylast, spreadw,
    parts, parts_in, v,
    turned, land_a, stage, land_b, scales,
    halo_ss, halo_rs, back_ss, back_rs, meta_ss, meta_rs, part_ss, part_rs, v_ss, v_rs,
    a_ss, a_rs, b_ss, b_rs, load_sem, control_sem,
):
    levels, height, width = control_ref.shape
    slots = meta.shape[2]
    chunks, pairs = slots // CHUNK, slots // (2 * CHUNK)
    size = levels // GROUPS
    rows = size * height
    lon, lat = lax.axis_index("lon"), lax.axis_index("lat")
    sides = [{"lon": lax.rem(lon + n_lon - 1, n_lon), "lat": lat}, {"lon": lax.rem(lon + 1, n_lon), "lat": lat}]
    ends = [({"lon": lon, "lat": lat - 1}, lat > 0), ({"lon": lon, "lat": lat + 1}, lat < n_lat - 1)]

    barrier = pltpu.get_barrier_semaphore()

    @pl.loop(1, n_lon)
    def _(d):
        pl.semaphore_signal(barrier, inc=1, device_id={"lon": lax.rem(lon + d, n_lon), "lat": lat})

    @pl.loop(1, n_lat)
    def _(d):
        pl.semaphore_signal(barrier, inc=1, device_id={"lon": lon, "lat": lax.rem(lat + d, n_lat)})

    far = [innov_far, ivar_far, mask_far, row_far, col_far, frow_far, fcol_far, counts_far, std_far]
    near = [innov_ref, ivar_ref, mask_ref, row_ref, col_ref, frow_ref, fcol_ref, counts_ref, std_ref]
    loads = [pltpu.make_async_copy(a, b, load_sem.at[i]) for i, (a, b) in enumerate(zip(far, near))]
    at_group = [pl.ds(g * size, size) for g in range(GROUPS)]
    control_loads = [
        pltpu.make_async_copy(control_far.at[at], control_ref.at[at], control_sem.at[g])
        for g, at in enumerate(at_group)
    ]
    for load in loads[:3] + control_loads + loads[3:]:
        load.start()

    def masked(g):
        part = control_ref[pl.ds(g * size, size)] * mask_ref[...].astype(F32)[None]
        return part.reshape(rows, width)

    def side_copy(out, landed, ss, rs, g, d):
        return pltpu.make_async_remote_copy(
            src_ref=out.at[d, g], dst_ref=landed.at[1 - d, g],
            send_sem=ss.at[d, g], recv_sem=rs.at[1 - d, g], device_id=sides[d],
        )

    def side_wait(out, landed, ss, rs, g):
        for d in range(2):
            pltpu.make_async_remote_copy(
                src_ref=out.at[d, g], dst_ref=landed.at[d, g],
                send_sem=ss.at[d, g], recv_sem=rs.at[d, g], device_id=sides[d],
            ).wait_recv()

    def pack_sides(x, out, g):
        out[0, g] = pack(x, 0)
        out[1, g] = pack(x, width - HALF)

    def halo_pack(g):
        pack_sides(masked(g), halo_out, g)

    def halo_send(g):
        for d in range(2):
            side_copy(halo_out, halo_in, halo_ss, halo_rs, g, d).start()

    deep = 2 * levels // n_lon
    loads[0].wait()
    loads[1].wait()
    blocks = []
    for i in range(n_lon):
        g, place = i * deep // (2 * size), i * deep % (2 * size)
        source, first = (innov_ref, ivar_ref)[place // size], g * size + place % size
        blocks.append(jnp.concatenate([source[first : first + deep, p, :] for p in range(n_lat)], axis=0))
    for q, block in enumerate(swap_blocks(blocks)):
        turned[q] = block

    loads[2].wait()
    control_loads[0].wait()
    halo_pack(0)
    pl.semaphore_wait(barrier, n_lon - 1 + n_lat - 1)

    def first_copy(d):
        return pltpu.make_async_remote_copy(
            src_ref=turned.at[lax.rem(lon + d, n_lon)], dst_ref=land_a.at[lon],
            send_sem=a_ss.at[d], recv_sem=a_rs.at[d],
            device_id={"lon": lax.rem(lon + d, n_lon), "lat": lat},
        )

    def first_wait(d):
        source = lax.rem(lon + n_lon - d, n_lon)
        pltpu.make_async_remote_copy(
            src_ref=turned.at[source], dst_ref=land_a.at[source],
            send_sem=a_ss.at[d], recv_sem=a_rs.at[d],
            device_id={"lon": source, "lat": lat},
        ).wait_recv()

    @pl.loop(1, n_lon)
    def _(d):
        first_copy(d).start()

    halo_send(0)
    land_a[pl.ds(lon, 1)] = turned[pl.ds(lon, 1)]

    for load in loads[3:]:
        load.wait()
    describe(mask_ref, row_ref, col_ref, frow_ref, fcol_ref, counts_ref, meta.at[1])

    def end_copy(src, dst, send_sem, recv_sem, d):
        return pltpu.make_async_remote_copy(
            src_ref=src, dst_ref=dst, send_sem=send_sem, recv_sem=recv_sem, device_id=ends[d][0]
        )

    def at_ends(body):
        for d in range(2):
            pl.when(ends[d][1])(functools.partial(body, d))

    def meta_copy(d):
        return end_copy(meta.at[1], meta.at[2 * (1 - d)], meta_ss.at[d], meta_rs.at[1 - d], d)

    at_ends(lambda d: meta_copy(d).start())
    for load in control_loads[1:]:
        load.wait()

    @pl.loop(1, GROUPS)
    def _(g):
        halo_pack(g)
        halo_send(g)


    for d in range(2):

        @pl.when(jnp.logical_not(ends[d][1]))
        def _():
            meta[2 * d] = jnp.zeros(meta.shape[1:], F32)
            v[2 * d] = jnp.zeros(v.shape[1:], F32)
            parts_in[d] = jnp.zeros(parts_in.shape[1:], F32)

    flat = jnp.concatenate([std_ref[i : i + 1, :] for i in range(std_ref.shape[0])], axis=1)
    eye = iota((levels, levels), 0) == iota((levels, levels), 1)
    scales[...] = jnp.sum(jnp.where(eye, flat, 0.0), axis=1, keepdims=True)

    k = iota((2 * width, width), 0)
    place = jnp.where(k < width, k, jnp.where(k < width + HALF, k - (width + HALF), k - HALF))
    place = jnp.where(k < width + 2 * HALF, place, 1000.0)
    ghi, glo = split(taps(place - iota((2 * width, width), 1)))
    filt[:, 0:width] = ghi
    filt[:, width : 2 * width] = glo

    def tables(t):
        shift = jnp.asarray((t - 1) * height, jnp.int32).astype(F32)

        @pl.loop(0, chunks, unroll=4)
        def _(c):
            at = pl.ds(pl.multiple_of(c * CHUNK, CHUNK), CHUNK)
            m = meta[t, :, at]
            y = m[0:1] + shift - iota((height, CHUNK), 0)
            near, far = taps(y), taps(y + 1.0)
            weight[t, c, :, 0:CHUNK] = m[2:3] * near + m[4:5] * far
            weight[t, c, :, CHUNK : 2 * CHUNK] = m[3:4] * near + m[5:6] * far
            ytap[t, :, at] = near
            ylast[t, :, at] = taps(m[0:1] + (shift + 1.0) + 0.0 * iota((8, CHUNK), 0))
            x = iota((width, CHUNK), 0) - m[1:2]
            onehot[t, c, :, 0:CHUNK] = jnp.where(x == 0.0, 1.0, 0.0).astype(BF16)
            onehot[t, c, :, CHUNK : 2 * CHUNK] = jnp.where(x == 1.0, 1.0, 0.0).astype(BF16)
            turn = jnp.transpose(m)
            x = iota((CHUNK, width), 1) - turn[:, 1:2]
            w = jnp.concatenate(
                [
                    jnp.where(x == 0.0, turn[:, 2 + 2 * i : 3 + 2 * i], 0.0)
                    + jnp.where(x == 1.0, turn[:, 3 + 2 * i : 4 + 2 * i], 0.0)
                    for i in range(2)
                ],
                axis=1,
            )
            hi, lo = split(w)
            spreadw[t, 0, at, :] = hi
            spreadw[t, 1, at, :] = lo

    tables(1)

    @pl.loop(1, n_lon)
    def _(d):
        first_wait(d)

    for i, block in enumerate(swap_blocks([land_a[t] for t in range(n_lon)])):
        for p in range(n_lat):
            stage[p, i * deep : (i + 1) * deep] = block[p * deep : (p + 1) * deep]

    def second_copy(o, d, source, target):
        at = pl.ds(pl.multiple_of(o * 2 * size, size), 2 * size)
        return pltpu.make_async_remote_copy(
            src_ref=stage.at[source, at], dst_ref=land_b.at[target, at],
            send_sem=b_ss.at[o, d], recv_sem=b_rs.at[o, d],
            device_id={"lon": lon, "lat": source},
        )

    def second_send(o, d):
        return second_copy(o, d, lax.rem(lat + d, n_lat), lat)

    @pl.loop(0, GROUPS)
    def _(o):
        @pl.loop(1, n_lat)
        def _(d):
            second_send(o, d).start()

    land_b[pl.ds(lat, 1)] = stage[pl.ds(lat, 1)]

    at_ends(lambda d: end_copy(meta.at[1], meta.at[2 * d], meta_ss.at[d], meta_rs.at[d], d).wait_recv())

    @pl.loop(0, 2)
    def _(d):
        tables(2 * d)

    def take_observations(o):
        @pl.loop(1, n_lat)
        def _(d):
            source = lax.rem(lat + n_lat - d, n_lat)
            second_copy(o, d, source, source).wait_recv()

    def smooth(x, beyond):
        hi, lo = split(jnp.concatenate([x, beyond], axis=1))
        wide = dot(hi, filt[...])
        return wide[:, :width] + wide[:, width:] + dot(lo, filt[:, 0:width])

    def part_copy(g, d):
        return end_copy(parts.at[2 * d, g], parts_in.at[1 - d, g], part_ss.at[d, g], part_rs.at[1 - d, g], d)

    def forward(g):
        side_wait(halo_out, halo_in, halo_ss, halo_rs, g)
        hi, lo = split(smooth(masked(g), unpack(halo_in[0, g], halo_in[1, g], rows)))
        ahl[:, 0:width] = hi
        ahl[:, width : 2 * width] = lo
        def gather(t, c):
            one = onehot[t, c]
            wide = dot(ahl[...], jnp.concatenate([one, one], axis=0))
            total = jnp.sum(wide.reshape(size, height, 2 * CHUNK) * weight[t, c][None], axis=1)
            at = pl.ds(pl.multiple_of(c * CHUNK, CHUNK), CHUNK)
            parts[t, g, :, at] = total[:, :CHUNK] + total[:, CHUNK:]

        @pl.loop(0, 3)
        def _(k):
            t = lax.rem(2 * k, 3)

            @pl.loop(0, chunks, unroll=4)
            def _(c):
                gather(t, c)

            @pl.when(k == 1)
            def _():
                at_ends(lambda d: part_copy(g, d).start())

    def v_copy(g, d):
        return end_copy(v.at[1, g], v.at[2 * (1 - d), g], v_ss.at[d, g], v_rs.at[1 - d, g], d)

    def misfit(g):
        at_ends(
            lambda d: end_copy(
                parts.at[2 * d, g], parts_in.at[d, g], part_ss.at[d, g], part_rs.at[d, g], d
            ).wait_recv()
        )
        scale = scales[pl.ds(pl.multiple_of(g * size, size), size), :]
        total = parts[1, g] + parts_in[0, g] + parts_in[1, g]
        take_observations(g)
        innov, ivar = (
            jnp.concatenate(
                [land_b[s, pl.ds(pl.multiple_of((2 * g + k) * size, size), size), :] for s in range(n_lat)], axis=1
            )
            for k in range(2)
        )
        v[1, g] = scale * ivar * (scale * total - innov)
        at_ends(lambda d: v_copy(g, d).start())

    def backward(g):
        at_ends(
            lambda d: end_copy(v.at[1, g], v.at[2 * d, g], v_ss.at[d, g], v_rs.at[d, g], d).wait_recv()
        )
        grown[...] = jnp.zeros_like(grown)

        @pl.loop(0, 3 * pairs, unroll=6)
        def _(i):
            t, c = i // pairs, i % pairs
            at = pl.ds(pl.multiple_of(c * 2 * CHUNK, 2 * CHUNK), 2 * CHUNK)
            value = v[t, g, :, at]
            b = (value[:, None, :] * ytap[t, :, at][None]).reshape(rows, 2 * CHUNK)
            last = value * ylast[t, 0:1, at]
            spare = grown.shape[0] - rows - size
            extra = jnp.concatenate([last, jnp.zeros((spare, 2 * CHUNK), F32)], axis=0) if spare else last
            hi, lo = split(jnp.concatenate([b, extra], axis=0))
            whi, wlo = spreadw[t, 0, at, :], spreadw[t, 1, at, :]
            total = dot(jnp.concatenate([hi, lo, hi], axis=1), jnp.concatenate([whi, whi, wlo], axis=0))
            grown[...] += total

        below = pltpu.roll(grown[0:rows, width : 2 * width], 1, 0)
        first = grown[rows : rows + size, width : 2 * width]
        first = jnp.broadcast_to(first[:, None, :], (size, height, width)).reshape(rows, width)
        row = lax.broadcasted_iota(jnp.int32, (size, height, width), 1).reshape(rows, width)
        x = grown[0:rows, 0:width] + jnp.where(row == 0, first, below)
        field[g] = x
        pack_sides(x, back_out, g)
        for d in range(2):
            side_copy(back_out, back_in, back_ss, back_rs, g, d).start()

    def finish(g):
        side_wait(back_out, back_in, back_ss, back_rs, g)
        x = smooth(field[g], unpack(back_in[0, g], back_in[1, g], rows))
        at = pl.ds(g * size, size)
        out_ref[at] = mask_ref[...].astype(F32)[None] * x.reshape(size, height, width)

    @pl.loop(0, GROUPS + 2)
    def _(step):
        pl.when(step < GROUPS)(lambda: forward(step))
        pl.when((step >= 1) & (step < GROUPS + 1))(lambda: misfit(step - 1))
        pl.when(step >= 2)(lambda: backward(step - 2))

    @pl.loop(0, GROUPS)
    def _(g):
        finish(g)

    @pl.loop(0, GROUPS)
    def _(g):
        for d in range(2):
            side_copy(halo_out, halo_in, halo_ss, halo_rs, g, d).wait_send()
            side_copy(back_out, back_in, back_ss, back_rs, g, d).wait_send()
        at_ends(lambda d: part_copy(g, d).wait_send())
        at_ends(lambda d: v_copy(g, d).wait_send())
    at_ends(lambda d: meta_copy(d).wait_send())

    @pl.loop(1, n_lon)
    def _(d):
        first_copy(d).wait_send()

    @pl.loop(0, GROUPS)
    def _(o):
        @pl.loop(1, n_lat)
        def _(d):
            second_send(o, d).wait_send()


def shards(n_lon, n_lat, control, land_mask, std_dev, innovation, inverse_var, *slots_of):
    levels = control.shape[0] * control.shape[1]
    height, width = control.shape[2:]
    slots = slots_of[0].shape[0] * slots_of[0].shape[1]
    chunks = slots // CHUNK
    size = levels // GROUPS
    rows = size * height
    packed = packing(rows)[0]
    grown = -(-(rows + size) // 16) * 16
    deep = 2 * levels // n_lon
    dma = pltpu.SemaphoreType.DMA
    group = dma((2, GROUPS))
    sides = pltpu.VMEM((2, GROUPS, packed, width), F32)

    inputs = [
        control.reshape(levels, height, width), land_mask, std_dev, innovation, inverse_var, *slots_of,
    ]
    gradient = pl.pallas_call(
        functools.partial(kernel, n_lon, n_lat),
        out_shape=jax.ShapeDtypeStruct((levels, height, width), F32),
        in_specs=[HBM] * 10,
        out_specs=VMEM,
        scratch_shapes=[pltpu.VMEM(x.shape, x.dtype) for x in inputs] + [
            pltpu.VMEM((2 * width, 2 * width), BF16),
            sides, sides, sides, sides,
            pltpu.VMEM((rows, 2 * width), BF16),
            pltpu.VMEM((grown, 2 * width), F32),
            pltpu.VMEM((GROUPS, rows, width), F32),
            pltpu.VMEM((3, 8, slots), F32),
            pltpu.VMEM((3, chunks, width, 2 * CHUNK), BF16),
            pltpu.VMEM((3, chunks, height, 2 * CHUNK), F32),
            pltpu.VMEM((3, height, slots), F32),
            pltpu.VMEM((3, 8, slots), F32),
            pltpu.VMEM((3, 2, slots, 2 * width), BF16),
            pltpu.VMEM((3, GROUPS, size, slots), F32),
            pltpu.VMEM((2, GROUPS, size, slots), F32),
            pltpu.VMEM((3, GROUPS, size, slots), F32),
            pltpu.VMEM((n_lon, n_lat * deep, width), F32),
            pltpu.VMEM((n_lon, n_lat * deep, width), F32),
            pltpu.VMEM((n_lat, 2 * levels, width), F32),
            pltpu.VMEM((n_lat, 2 * levels, width), F32),
            pltpu.VMEM((levels, 1), F32),
            group, group, group, group, dma((2,)), dma((2,)), group, group, group, group,
            dma((n_lon,)), dma((n_lon,)), dma((GROUPS, n_lat)), dma((GROUPS, n_lat)),
            dma((9,)), dma((GROUPS,)),
        ],
        compiler_params=pltpu.CompilerParams(
            vmem_limit_bytes=56 << 20, collective_id=0, has_side_effects=True
        ),
        name="gradient",
    )(*inputs)
    return control + gradient.reshape(control.shape)


def solution(mesh):
    tile = P("lat", "lon")
    in_specs = (
        P(None, None, "lat", "lon"), tile, P(),
        P(None, "lat", "lon"), P(None, "lat", "lon"),
        tile, tile, tile, tile, tile,
    )
    body = functools.partial(shards, mesh.shape["lon"], mesh.shape["lat"])
    return jax.shard_map(
        body, mesh=mesh, in_specs=in_specs,
        out_specs=P(None, None, "lat", "lon"), check_vma=False,
    )
```

```python
import functools

import jax
import jax.numpy as jnp
import numpy as np
from jax import lax
from jax.experimental import pallas as pl
from jax.experimental.pallas import tpu as pltpu
from jax.sharding import PartitionSpec as P

HALF = 50
SPREAD = HALF / 2.0
_TAPS = np.exp(-0.5 * (np.arange(-HALF, HALF + 1) / SPREAD) ** 2)
NORM = float(1.0 / np.sqrt(np.sum(_TAPS * _TAPS)))
CHUNK = 128
GROUPS = 4
PIECE = HALF // 2
VMEM = pl.BlockSpec(memory_space=pltpu.VMEM)
HBM = pl.BlockSpec(memory_space=pltpu.HBM)
F32, BF16 = jnp.float32, jnp.bfloat16


def split(x):
    hi = x.astype(BF16)
    return hi, (x - hi.astype(F32)).astype(BF16)


def taps(distance):
    values = jnp.exp(distance * distance * (-0.5 / (SPREAD * SPREAD))) * NORM
    return jnp.where(jnp.abs(distance) < HALF + 0.5, values, 0.0)


def iota(shape, dim):
    return lax.broadcasted_iota(jnp.int32, shape, dim).astype(F32)


def dot(a, b):
    return jnp.dot(a, b, preferred_element_type=F32)


def roll(x, shift):
    shift = shift % x.shape[1]
    return pltpu.roll(x, shift, 1) if shift else x


def packing(rows):
    per = 128 // PIECE
    packed = -(-2 * rows // (8 * per)) * 8
    segments, at = [], 0
    while at < 2 * rows:
        half, row = at // rows, at % rows
        slot, place = at // packed, at % packed
        count = min(rows - row, packed - place)
        segments.append((half, row, count, slot, place))
        at += count
    return packed, segments


def pack(x, first):
    rows, width = x.shape
    packed, segments = packing(rows)
    lane = lax.broadcasted_iota(jnp.int32, (packed, width), 1)
    result = None
    for slot in range(segments[-1][3] + 1):
        mine = [s for s in segments if s[3] == slot]
        pieces = [
            roll(x[row : row + count], slot * PIECE - (first + half * PIECE))
            for half, row, count, _, _ in mine
        ]
        lacking = packed - sum(s[2] for s in mine)
        if lacking:
            pieces.append(x[:lacking])
        piece = jnp.concatenate(pieces, axis=0) if len(pieces) > 1 else pieces[0]
        result = piece if result is None else jnp.where(lane >= slot * PIECE, piece, result)
    return result


def unpack(left, right, rows):
    _, segments = packing(rows)
    lane = lax.broadcasted_iota(jnp.int32, (rows, left.shape[1]), 1)
    result = None
    for k, source in enumerate((left, right)):
        for half in range(2):
            target = k * HALF + half * PIECE
            pieces = [
                roll(source[place : place + count], target - slot * PIECE)
                for h, _, count, slot, place in segments
                if h == half
            ]
            piece = jnp.concatenate(pieces, axis=0)
            result = piece if result is None else jnp.where(lane >= target, piece, result)
    return result


def swap_blocks(blocks):
    count = len(blocks)
    width = blocks[0].shape[1] // count
    group = lax.broadcasted_iota(jnp.int32, blocks[0].shape, 1) // width
    bit = 1
    while bit < count:
        low = (group & bit) == 0
        fresh = []
        for k in range(count):
            other = blocks[k ^ bit]
            if k & bit == 0:
                fresh.append(jnp.where(low, blocks[k], roll(other, width * bit)))
            else:
                fresh.append(jnp.where(low, roll(other, -width * bit), blocks[k]))
        blocks = fresh
        bit *= 2
    return blocks


def describe(mask_ref, row_ref, col_ref, frow_ref, fcol_ref, counts_ref, out_ref):
    mask = mask_ref[...].astype(BF16)
    height, width = mask.shape
    holders, lanes = row_ref.shape
    tiles = counts_ref.shape[1]
    cap = lanes // tiles
    tile = lax.broadcasted_iota(jnp.int32, (tiles, lanes), 0)
    lane = lax.broadcasted_iota(jnp.int32, (tiles, lanes), 1)
    inside = (lane >= tile * cap) & (lane < tile * cap + cap)
    repeat = jnp.where(inside, 1.0, 0.0).astype(BF16)
    first = jnp.sum(jnp.where(inside, tile * cap, 0).astype(F32), axis=0, keepdims=True)
    number = iota((1, lanes), 1) - first
    limits = dot(counts_ref[...].astype(F32).astype(BF16), repeat)
    for s in range(holders):
        row = row_ref[pl.ds(s, 1), :].astype(F32)
        col = col_ref[pl.ds(s, 1), :].astype(F32)
        a = frow_ref[pl.ds(s, 1), :]
        b = fcol_ref[pl.ds(s, 1), :]
        x = iota((width, lanes), 0) - col
        both = jnp.concatenate(
            [jnp.where(x == 0.0, 1.0, 0.0).astype(BF16), jnp.where(x == 1.0, 1.0, 0.0).astype(BF16)], axis=1
        )
        found = dot(mask, both)
        left, right = found[:, :lanes], found[:, lanes:]
        y = iota((height, lanes), 0) - row
        m00 = jnp.sum(jnp.where(y == 0.0, left, 0.0), axis=0, keepdims=True)
        m01 = jnp.sum(jnp.where(y == 0.0, right, 0.0), axis=0, keepdims=True)
        m10 = jnp.sum(jnp.where(y == 1.0, left, 0.0), axis=0, keepdims=True)
        m11 = jnp.sum(jnp.where(y == 1.0, right, 0.0), axis=0, keepdims=True)
        live = jnp.where(number < limits[s : s + 1], 1.0, 0.0)
        at = pl.ds(s * lanes, lanes)
        out_ref[0:1, at] = row
        out_ref[1:2, at] = col
        out_ref[2:3, at] = (1.0 - a) * (1.0 - b) * m00 * live
        out_ref[3:4, at] = (1.0 - a) * b * m01 * live
        out_ref[4:5, at] = a * (1.0 - b) * m10 * live
        out_ref[5:6, at] = a * b * m11 * live
        out_ref[6:7, at] = live
        out_ref[7:8, at] = live


def kernel(
    n_lon, n_lat,
    control_far, mask_far, std_far, innov_far, ivar_far, row_far, col_far, frow_far, fcol_far, counts_far,
    out_ref,
    control_ref, mask_ref, std_ref, innov_ref, ivar_ref, row_ref, col_ref, frow_ref, fcol_ref, counts_ref,
    filt, halo_out, halo_in, back_out, back_in, ahl, grown, field,
    meta, onehot, weight, ytap, ylast, spreadw,
    parts, parts_in, v,
    turned, land_a, stage, land_b, scales,
    halo_ss, halo_rs, back_ss, back_rs, meta_ss, meta_rs, part_ss, part_rs, v_ss, v_rs,
    a_ss, a_rs, b_ss, b_rs, load_sem, control_sem,
):
    levels, height, width = control_ref.shape
    slots = meta.shape[2]
    chunks, pairs = slots // CHUNK, slots // (2 * CHUNK)
    size = levels // GROUPS
    rows = size * height
    lon, lat = lax.axis_index("lon"), lax.axis_index("lat")
    sides = [{"lon": lax.rem(lon + n_lon - 1, n_lon), "lat": lat}, {"lon": lax.rem(lon + 1, n_lon), "lat": lat}]
    ends = [({"lon": lon, "lat": lat - 1}, lat > 0), ({"lon": lon, "lat": lat + 1}, lat < n_lat - 1)]

    barrier = pltpu.get_barrier_semaphore()

    @pl.loop(1, n_lon)
    def _(d):
        pl.semaphore_signal(barrier, inc=1, device_id={"lon": lax.rem(lon + d, n_lon), "lat": lat})

    @pl.loop(1, n_lat)
    def _(d):
        pl.semaphore_signal(barrier, inc=1, device_id={"lon": lon, "lat": lax.rem(lat + d, n_lat)})

    far = [innov_far, ivar_far, mask_far, row_far, col_far, frow_far, fcol_far, counts_far, std_far]
    near = [innov_ref, ivar_ref, mask_ref, row_ref, col_ref, frow_ref, fcol_ref, counts_ref, std_ref]
    loads = [pltpu.make_async_copy(a, b, load_sem.at[i]) for i, (a, b) in enumerate(zip(far, near))]
    at_group = [pl.ds(g * size, size) for g in range(GROUPS)]
    control_loads = [
        pltpu.make_async_copy(control_far.at[at], control_ref.at[at], control_sem.at[g])
        for g, at in enumerate(at_group)
    ]
    for load in loads[:3] + control_loads + loads[3:]:
        load.start()

    def masked(g):
        part = control_ref[pl.ds(g * size, size)] * mask_ref[...].astype(F32)[None]
        return part.reshape(rows, width)

    def side_copy(out, landed, ss, rs, g, d):
        return pltpu.make_async_remote_copy(
            src_ref=out.at[d, g], dst_ref=landed.at[1 - d, g],
            send_sem=ss.at[0], recv_sem=rs.at[1 - d, g], device_id=sides[d],
        )

    def side_wait(out, landed, ss, rs, g):
        for d in range(2):
            pltpu.make_async_remote_copy(
                src_ref=out.at[d, g], dst_ref=landed.at[d, g],
                send_sem=ss.at[0], recv_sem=rs.at[d, g], device_id=sides[d],
            ).wait_recv()

    def pack_sides(x, out, g):
        out[0, g] = pack(x, 0)
        out[1, g] = pack(x, width - HALF)

    def halo_pack(g):
        pack_sides(masked(g), halo_out, g)

    def halo_send(g):
        for d in range(2):
            side_copy(halo_out, halo_in, halo_ss, halo_rs, g, d).start()

    deep = 2 * levels // n_lon
    loads[0].wait()
    loads[1].wait()
    blocks = []
    for i in range(n_lon):
        g, place = i * deep // (2 * size), i * deep % (2 * size)
        source, first = (innov_ref, ivar_ref)[place // size], g * size + place % size
        blocks.append(jnp.concatenate([source[first : first + deep, p, :] for p in range(n_lat)], axis=0))
    for q, block in enumerate(swap_blocks(blocks)):
        turned[q] = block

    loads[2].wait()
    control_loads[0].wait()
    halo_pack(0)
    pl.semaphore_wait(barrier, n_lon - 1 + n_lat - 1)

    def first_copy(d):
        return pltpu.make_async_remote_copy(
            src_ref=turned.at[lax.rem(lon + d, n_lon)], dst_ref=land_a.at[lon],
            send_sem=a_ss.at[0], recv_sem=a_rs.at[0],
            device_id={"lon": lax.rem(lon + d, n_lon), "lat": lat},
        )

    def first_all():
        every = pl.ds(0, n_lon - 1)
        return pltpu.make_async_remote_copy(
            src_ref=turned.at[every], dst_ref=land_a.at[every],
            send_sem=a_ss.at[0], recv_sem=a_rs.at[0], device_id=sides[1],
        )

    @pl.loop(1, n_lon)
    def _(d):
        first_copy(d).start()

    halo_send(0)
    land_a[pl.ds(lon, 1)] = turned[pl.ds(lon, 1)]

    for load in loads[3:]:
        load.wait()
    describe(mask_ref, row_ref, col_ref, frow_ref, fcol_ref, counts_ref, meta.at[1])

    def end_copy(src, dst, send_sem, recv_sem, d):
        return pltpu.make_async_remote_copy(
            src_ref=src, dst_ref=dst, send_sem=send_sem, recv_sem=recv_sem, device_id=ends[d][0]
        )

    def at_ends(body):
        for d in range(2):
            pl.when(ends[d][1])(functools.partial(body, d))

    def meta_copy(d):
        return end_copy(meta.at[1], meta.at[2 * (1 - d)], meta_ss.at[d], meta_rs.at[1 - d], d)

    at_ends(lambda d: meta_copy(d).start())
    for load in control_loads[1:]:
        load.wait()

    @pl.loop(1, GROUPS)
    def _(g):
        halo_pack(g)
        halo_send(g)


    for d in range(2):

        @pl.when(jnp.logical_not(ends[d][1]))
        def _():
            meta[2 * d] = jnp.zeros(meta.shape[1:], F32)
            v[2 * d] = jnp.zeros(v.shape[1:], F32)
            parts_in[d] = jnp.zeros(parts_in.shape[1:], F32)

    flat = jnp.concatenate([std_ref[i : i + 1, :] for i in range(std_ref.shape[0])], axis=1)
    eye = iota((levels, levels), 0) == iota((levels, levels), 1)
    scales[...] = jnp.sum(jnp.where(eye, flat, 0.0), axis=1, keepdims=True)

    k = iota((2 * width, width), 0)
    place = jnp.where(k < width, k, jnp.where(k < width + HALF, k - (width + HALF), k - HALF))
    place = jnp.where(k < width + 2 * HALF, place, 1000.0)
    ghi, glo = split(taps(place - iota((2 * width, width), 1)))
    filt[:, 0:width] = ghi
    filt[:, width : 2 * width] = glo

    def tables(t):
        shift = jnp.asarray((t - 1) * height, jnp.int32).astype(F32)

        @pl.loop(0, chunks, unroll=4)
        def _(c):
            at = pl.ds(pl.multiple_of(c * CHUNK, CHUNK), CHUNK)
            m = meta[t, :, at]
            y = m[0:1] + shift - iota((height, CHUNK), 0)
            near, far = taps(y), taps(y + 1.0)
            weight[t, c, :, 0:CHUNK] = m[2:3] * near + m[4:5] * far
            weight[t, c, :, CHUNK : 2 * CHUNK] = m[3:4] * near + m[5:6] * far
            ytap[t, :, at] = near
            ylast[t, :, at] = taps(m[0:1] + (shift + 1.0) + 0.0 * iota((8, CHUNK), 0))
            x = iota((width, CHUNK), 0) - m[1:2]
            onehot[t, c, :, 0:CHUNK] = jnp.where(x == 0.0, 1.0, 0.0).astype(BF16)
            onehot[t, c, :, CHUNK : 2 * CHUNK] = jnp.where(x == 1.0, 1.0, 0.0).astype(BF16)
            turn = jnp.transpose(m)
            x = iota((CHUNK, width), 1) - turn[:, 1:2]
            w = jnp.concatenate(
                [
                    jnp.where(x == 0.0, turn[:, 2 + 2 * i : 3 + 2 * i], 0.0)
                    + jnp.where(x == 1.0, turn[:, 3 + 2 * i : 4 + 2 * i], 0.0)
                    for i in range(2)
                ],
                axis=1,
            )
            hi, lo = split(w)
            spreadw[t, 0, at, :] = hi
            spreadw[t, 1, at, :] = lo

    tables(1)

    first_all().wait_recv()

    for i, block in enumerate(swap_blocks([land_a[t] for t in range(n_lon)])):
        for p in range(n_lat):
            stage[p, i * deep : (i + 1) * deep] = block[p * deep : (p + 1) * deep]

    def second_copy(o, d, source, target):
        at = pl.ds(pl.multiple_of(o * 2 * size, size), 2 * size)
        return pltpu.make_async_remote_copy(
            src_ref=stage.at[source, at], dst_ref=land_b.at[target, at],
            send_sem=b_ss.at[0], recv_sem=b_rs.at[o],
            device_id={"lon": lon, "lat": source},
        )

    def second_send(o, d):
        return second_copy(o, d, lax.rem(lat + d, n_lat), lat)

    @pl.loop(0, GROUPS)
    def _(o):
        @pl.loop(1, n_lat)
        def _(d):
            second_send(o, d).start()

    land_b[pl.ds(lat, 1)] = stage[pl.ds(lat, 1)]

    at_ends(lambda d: end_copy(meta.at[1], meta.at[2 * d], meta_ss.at[d], meta_rs.at[d], d).wait_recv())

    @pl.loop(0, 2)
    def _(d):
        tables(2 * d)

    def take_observations(o):
        every, at = pl.ds(0, n_lat - 1), pl.ds(pl.multiple_of(o * 2 * size, size), 2 * size)
        pltpu.make_async_remote_copy(
            src_ref=stage.at[every, at], dst_ref=land_b.at[every, at],
            send_sem=b_ss.at[0], recv_sem=b_rs.at[o], device_id=sides[1],
        ).wait_recv()

    def smooth(x, beyond):
        hi, lo = split(jnp.concatenate([x, beyond], axis=1))
        wide = dot(hi, filt[...])
        return wide[:, :width] + wide[:, width:] + dot(lo, filt[:, 0:width])

    def part_copy(g, d):
        return end_copy(parts.at[2 * d, g], parts_in.at[1 - d, g], part_ss.at[d], part_rs.at[1 - d, g], d)

    def forward(g):
        side_wait(halo_out, halo_in, halo_ss, halo_rs, g)
        hi, lo = split(smooth(masked(g), unpack(halo_in[0, g], halo_in[1, g], rows)))
        ahl[:, 0:width] = hi
        ahl[:, width : 2 * width] = lo
        def gather(t, c):
            one = onehot[t, c]
            wide = dot(ahl[...], jnp.concatenate([one, one], axis=0))
            total = jnp.sum(wide.reshape(size, height, 2 * CHUNK) * weight[t, c][None], axis=1)
            at = pl.ds(pl.multiple_of(c * CHUNK, CHUNK), CHUNK)
            parts[t, g, :, at] = total[:, :CHUNK] + total[:, CHUNK:]

        @pl.loop(0, 3)
        def _(k):
            t = lax.rem(2 * k, 3)

            @pl.loop(0, chunks, unroll=4)
            def _(c):
                gather(t, c)

            @pl.when(k == 1)
            def _():
                at_ends(lambda d: part_copy(g, d).start())

    def v_copy(g, d):
        return end_copy(v.at[1, g], v.at[2 * (1 - d), g], v_ss.at[d], v_rs.at[1 - d, g], d)

    def misfit(g):
        at_ends(
            lambda d: end_copy(
                parts.at[2 * d, g], parts_in.at[d, g], part_ss.at[d], part_rs.at[d, g], d
            ).wait_recv()
        )
        scale = scales[pl.ds(pl.multiple_of(g * size, size), size), :]
        total = parts[1, g] + parts_in[0, g] + parts_in[1, g]
        take_observations(g)
        innov, ivar = (
            jnp.concatenate(
                [land_b[s, pl.ds(pl.multiple_of((2 * g + k) * size, size), size), :] for s in range(n_lat)], axis=1
            )
            for k in range(2)
        )
        v[1, g] = scale * ivar * (scale * total - innov)
        at_ends(lambda d: v_copy(g, d).start())

    def backward(g):
        at_ends(
            lambda d: end_copy(v.at[1, g], v.at[2 * d, g], v_ss.at[d], v_rs.at[d, g], d).wait_recv()
        )
        grown[...] = jnp.zeros_like(grown)

        @pl.loop(0, 3 * pairs, unroll=6)
        def _(i):
            t, c = i // pairs, i % pairs
            at = pl.ds(pl.multiple_of(c * 2 * CHUNK, 2 * CHUNK), 2 * CHUNK)
            value = v[t, g, :, at]
            b = (value[:, None, :] * ytap[t, :, at][None]).reshape(rows, 2 * CHUNK)
            last = value * ylast[t, 0:1, at]
            spare = grown.shape[0] - rows - size
            extra = jnp.concatenate([last, jnp.zeros((spare, 2 * CHUNK), F32)], axis=0) if spare else last
            hi, lo = split(jnp.concatenate([b, extra], axis=0))
            whi, wlo = spreadw[t, 0, at, :], spreadw[t, 1, at, :]
            total = dot(jnp.concatenate([hi, lo, hi], axis=1), jnp.concatenate([whi, whi, wlo], axis=0))
            grown[...] += total

        below = pltpu.roll(grown[0:rows, width : 2 * width], 1, 0)
        first = grown[rows : rows + size, width : 2 * width]
        first = jnp.broadcast_to(first[:, None, :], (size, height, width)).reshape(rows, width)
        row = lax.broadcasted_iota(jnp.int32, (size, height, width), 1).reshape(rows, width)
        x = grown[0:rows, 0:width] + jnp.where(row == 0, first, below)
        field[g] = x
        pack_sides(x, back_out, g)
        for d in range(2):
            side_copy(back_out, back_in, back_ss, back_rs, g, d).start()

    def finish(g):
        side_wait(back_out, back_in, back_ss, back_rs, g)
        x = smooth(field[g], unpack(back_in[0, g], back_in[1, g], rows))
        at = pl.ds(g * size, size)
        out_ref[at] = mask_ref[...].astype(F32)[None] * x.reshape(size, height, width)

    @pl.loop(0, GROUPS + 2)
    def _(step):
        pl.when(step < GROUPS)(lambda: forward(step))
        pl.when((step >= 1) & (step < GROUPS + 1))(lambda: misfit(step - 1))
        pl.when(step >= 2)(lambda: backward(step - 2))

    @pl.loop(0, GROUPS)
    def _(g):
        finish(g)

    def all_sent(source, sem):
        pltpu.make_async_remote_copy(
            src_ref=source, dst_ref=source, send_sem=sem, recv_sem=sem, device_id=sides[1]
        ).wait_send()

    all_sent(halo_out, halo_ss.at[0])
    all_sent(back_out, back_ss.at[0])
    all_sent(turned.at[pl.ds(0, n_lon - 1)], a_ss.at[0])
    all_sent(stage.at[pl.ds(0, n_lat - 1)], b_ss.at[0])

    def ends_sent(d):
        all_sent(parts.at[2 * d], part_ss.at[d])
        all_sent(v.at[1], v_ss.at[d])
        meta_copy(d).wait_send()

    at_ends(ends_sent)


def shards(n_lon, n_lat, control, land_mask, std_dev, innovation, inverse_var, *slots_of):
    levels = control.shape[0] * control.shape[1]
    height, width = control.shape[2:]
    slots = slots_of[0].shape[0] * slots_of[0].shape[1]
    chunks = slots // CHUNK
    size = levels // GROUPS
    rows = size * height
    packed = packing(rows)[0]
    grown = -(-(rows + size) // 16) * 16
    deep = 2 * levels // n_lon
    dma = pltpu.SemaphoreType.DMA
    group, both, one = dma((2, GROUPS)), dma((2,)), dma((1,))
    sides = pltpu.VMEM((2, GROUPS, packed, width), F32)

    inputs = [
        control.reshape(levels, height, width), land_mask, std_dev, innovation, inverse_var, *slots_of,
    ]
    gradient = pl.pallas_call(
        functools.partial(kernel, n_lon, n_lat),
        out_shape=pltpu.VMEM((levels, height, width), F32),
        in_specs=[HBM] * 10,
        out_specs=VMEM,
        scratch_shapes=[pltpu.VMEM(x.shape, x.dtype) for x in inputs] + [
            pltpu.VMEM((2 * width, 2 * width), BF16),
            sides, sides, sides, sides,
            pltpu.VMEM((rows, 2 * width), BF16),
            pltpu.VMEM((grown, 2 * width), F32),
            pltpu.VMEM((GROUPS, rows, width), F32),
            pltpu.VMEM((3, 8, slots), F32),
            pltpu.VMEM((3, chunks, width, 2 * CHUNK), BF16),
            pltpu.VMEM((3, chunks, height, 2 * CHUNK), F32),
            pltpu.VMEM((3, height, slots), F32),
            pltpu.VMEM((3, 8, slots), F32),
            pltpu.VMEM((3, 2, slots, 2 * width), BF16),
            pltpu.VMEM((3, GROUPS, size, slots), F32),
            pltpu.VMEM((2, GROUPS, size, slots), F32),
            pltpu.VMEM((3, GROUPS, size, slots), F32),
            pltpu.VMEM((n_lon, n_lat * deep, width), F32),
            pltpu.VMEM((n_lon, n_lat * deep, width), F32),
            pltpu.VMEM((n_lat, 2 * levels, width), F32),
            pltpu.VMEM((n_lat, 2 * levels, width), F32),
            pltpu.VMEM((levels, 1), F32),
            one, group, one, group, both, both, both, group, both, group, one, one, one, dma((GROUPS,)),
            dma((9,)), dma((GROUPS,)),
        ],
        compiler_params=pltpu.CompilerParams(
            vmem_limit_bytes=56 << 20, collective_id=0, has_side_effects=True
        ),
        name="gradient",
    )(*inputs)
    return control + gradient.reshape(control.shape)


def solution(mesh):
    tile = P("lat", "lon")
    in_specs = (
        P(None, None, "lat", "lon"), tile, P(),
        P(None, "lat", "lon"), P(None, "lat", "lon"),
        tile, tile, tile, tile, tile,
    )
    body = functools.partial(shards, mesh.shape["lon"], mesh.shape["lat"])
    return jax.shard_map(
        body, mesh=mesh, in_specs=in_specs,
        out_specs=P(None, None, "lat", "lon"), check_vma=False,
    )
```

```python
import functools

import jax
import jax.numpy as jnp
import numpy as np
from jax import lax
from jax.experimental import pallas as pl
from jax.experimental.pallas import tpu as pltpu
from jax.sharding import PartitionSpec as P

HALF = 50
SPREAD = HALF / 2.0
_TAPS = np.exp(-0.5 * (np.arange(-HALF, HALF + 1) / SPREAD) ** 2)
NORM = float(1.0 / np.sqrt(np.sum(_TAPS * _TAPS)))
CHUNK = 128
GROUPS = 4
PIECE = HALF // 2
VMEM = pl.BlockSpec(memory_space=pltpu.VMEM)
HBM = pl.BlockSpec(memory_space=pltpu.HBM)
F32, BF16 = jnp.float32, jnp.bfloat16


def split(x):
    hi = x.astype(BF16)
    return hi, (x - hi.astype(F32)).astype(BF16)


def taps(distance):
    values = jnp.exp(distance * distance * (-0.5 / (SPREAD * SPREAD))) * NORM
    return jnp.where(jnp.abs(distance) < HALF + 0.5, values, 0.0)


def iota(shape, dim):
    return lax.broadcasted_iota(jnp.int32, shape, dim).astype(F32)


def dot(a, b):
    return jnp.dot(a, b, preferred_element_type=F32)


def roll(x, shift):
    shift = shift % x.shape[1]
    return pltpu.roll(x, shift, 1) if shift else x


def packing(rows):
    per = 128 // PIECE
    packed = -(-2 * rows // (8 * per)) * 8
    segments, at = [], 0
    while at < 2 * rows:
        half, row = at // rows, at % rows
        slot, place = at // packed, at % packed
        count = min(rows - row, packed - place)
        segments.append((half, row, count, slot, place))
        at += count
    return packed, segments


def pack(x, first):
    rows, width = x.shape
    packed, segments = packing(rows)
    lane = lax.broadcasted_iota(jnp.int32, (packed, width), 1)
    result = None
    for slot in range(segments[-1][3] + 1):
        mine = [s for s in segments if s[3] == slot]
        pieces = [
            roll(x[row : row + count], slot * PIECE - (first + half * PIECE))
            for half, row, count, _, _ in mine
        ]
        lacking = packed - sum(s[2] for s in mine)
        if lacking:
            pieces.append(x[:lacking])
        piece = jnp.concatenate(pieces, axis=0) if len(pieces) > 1 else pieces[0]
        result = piece if result is None else jnp.where(lane >= slot * PIECE, piece, result)
    return result


def unpack(left, right, rows):
    _, segments = packing(rows)
    lane = lax.broadcasted_iota(jnp.int32, (rows, left.shape[1]), 1)
    result = None
    for k, source in enumerate((left, right)):
        for half in range(2):
            target = k * HALF + half * PIECE
            pieces = [
                roll(source[place : place + count], target - slot * PIECE)
                for h, _, count, slot, place in segments
                if h == half
            ]
            piece = jnp.concatenate(pieces, axis=0)
            result = piece if result is None else jnp.where(lane >= target, piece, result)
    return result


def swap_blocks(blocks):
    count = len(blocks)
    width = blocks[0].shape[1] // count
    group = lax.broadcasted_iota(jnp.int32, blocks[0].shape, 1) // width
    bit = 1
    while bit < count:
        low = (group & bit) == 0
        fresh = []
        for k in range(count):
            other = blocks[k ^ bit]
            if k & bit == 0:
                fresh.append(jnp.where(low, blocks[k], roll(other, width * bit)))
            else:
                fresh.append(jnp.where(low, roll(other, -width * bit), blocks[k]))
        blocks = fresh
        bit *= 2
    return blocks


def describe(mask_ref, row_ref, col_ref, frow_ref, fcol_ref, counts_ref, out_ref):
    mask = mask_ref[...].astype(BF16)
    height, width = mask.shape
    holders, lanes = row_ref.shape
    tiles = counts_ref.shape[1]
    cap = lanes // tiles
    tile = lax.broadcasted_iota(jnp.int32, (tiles, lanes), 0)
    lane = lax.broadcasted_iota(jnp.int32, (tiles, lanes), 1)
    inside = (lane >= tile * cap) & (lane < tile * cap + cap)
    repeat = jnp.where(inside, 1.0, 0.0).astype(BF16)
    first = jnp.sum(jnp.where(inside, tile * cap, 0).astype(F32), axis=0, keepdims=True)
    number = iota((1, lanes), 1) - first
    limits = dot(counts_ref[...].astype(F32).astype(BF16), repeat)
    for s in range(holders):
        row = row_ref[pl.ds(s, 1), :].astype(F32)
        col = col_ref[pl.ds(s, 1), :].astype(F32)
        a = frow_ref[pl.ds(s, 1), :]
        b = fcol_ref[pl.ds(s, 1), :]
        x = iota((width, lanes), 0) - col
        both = jnp.concatenate(
            [jnp.where(x == 0.0, 1.0, 0.0).astype(BF16), jnp.where(x == 1.0, 1.0, 0.0).astype(BF16)], axis=1
        )
        found = dot(mask, both)
        left, right = found[:, :lanes], found[:, lanes:]
        y = iota((height, lanes), 0) - row
        m00 = jnp.sum(jnp.where(y == 0.0, left, 0.0), axis=0, keepdims=True)
        m01 = jnp.sum(jnp.where(y == 0.0, right, 0.0), axis=0, keepdims=True)
        m10 = jnp.sum(jnp.where(y == 1.0, left, 0.0), axis=0, keepdims=True)
        m11 = jnp.sum(jnp.where(y == 1.0, right, 0.0), axis=0, keepdims=True)
        live = jnp.where(number < limits[s : s + 1], 1.0, 0.0)
        at = pl.ds(s * lanes, lanes)
        out_ref[0:1, at] = row
        out_ref[1:2, at] = col
        out_ref[2:3, at] = (1.0 - a) * (1.0 - b) * m00 * live
        out_ref[3:4, at] = (1.0 - a) * b * m01 * live
        out_ref[4:5, at] = a * (1.0 - b) * m10 * live
        out_ref[5:6, at] = a * b * m11 * live
        out_ref[6:7, at] = live
        out_ref[7:8, at] = live


def kernel(
    n_lon, n_lat,
    control_far, mask_far, std_far, innov_far, ivar_far, row_far, col_far, frow_far, fcol_far, counts_far,
    out_ref,
    control_ref, mask_ref, std_ref, innov_ref, ivar_ref, row_ref, col_ref, frow_ref, fcol_ref, counts_ref,
    filt, halo_out, halo_in, back_out, back_in, ahl, grown, field,
    meta, onehot, weight, ytap, ylast, spreadw,
    parts, parts_in, v,
    turned, land_a, stage, land_b, scales,
    halo_ss, halo_rs, back_ss, back_rs, meta_ss, meta_rs, part_ss, part_rs, v_ss, v_rs,
    a_ss, a_rs, b_ss, b_rs, load_sem, control_sem,
):
    levels, height, width = control_ref.shape
    slots = meta.shape[2]
    chunks, pairs = slots // CHUNK, slots // (2 * CHUNK)
    size = levels // GROUPS
    rows = size * height
    lon, lat = lax.axis_index("lon"), lax.axis_index("lat")
    sides = [{"lon": lax.rem(lon + n_lon - 1, n_lon), "lat": lat}, {"lon": lax.rem(lon + 1, n_lon), "lat": lat}]
    ends = [({"lon": lon, "lat": lat - 1}, lat > 0), ({"lon": lon, "lat": lat + 1}, lat < n_lat - 1)]

    barrier = pltpu.get_barrier_semaphore()

    @pl.loop(1, n_lon)
    def _(d):
        pl.semaphore_signal(barrier, inc=1, device_id={"lon": lax.rem(lon + d, n_lon), "lat": lat})

    @pl.loop(1, n_lat)
    def _(d):
        pl.semaphore_signal(barrier, inc=1, device_id={"lon": lon, "lat": lax.rem(lat + d, n_lat)})

    far = [innov_far, ivar_far, mask_far, row_far, col_far, frow_far, fcol_far, counts_far, std_far]
    near = [innov_ref, ivar_ref, mask_ref, row_ref, col_ref, frow_ref, fcol_ref, counts_ref, std_ref]
    loads = [pltpu.make_async_copy(a, b, load_sem.at[i]) for i, (a, b) in enumerate(zip(far, near))]
    at_group = [pl.ds(g * size, size) for g in range(GROUPS)]
    control_loads = [
        pltpu.make_async_copy(control_far.at[at], control_ref.at[at], control_sem.at[g])
        for g, at in enumerate(at_group)
    ]
    for load in loads[:3] + control_loads + loads[3:]:
        load.start()

    def masked(g):
        part = control_ref[pl.ds(g * size, size)] * mask_ref[...].astype(F32)[None]
        return part.reshape(rows, width)

    def side_copy(out, landed, ss, rs, g, d):
        return pltpu.make_async_remote_copy(
            src_ref=out.at[d, g], dst_ref=landed.at[1 - d, g],
            send_sem=ss.at[0], recv_sem=rs.at[1 - d, g], device_id=sides[d],
        )

    def side_wait(out, landed, ss, rs, g):
        for d in range(2):
            pltpu.make_async_remote_copy(
                src_ref=out.at[d, g], dst_ref=landed.at[d, g],
                send_sem=ss.at[0], recv_sem=rs.at[d, g], device_id=sides[d],
            ).wait_recv()

    def pack_sides(x, out, g):
        out[0, g] = pack(x, 0)
        out[1, g] = pack(x, width - HALF)

    def halo_pack(g):
        pack_sides(masked(g), halo_out, g)

    def halo_send(g):
        for d in range(2):
            side_copy(halo_out, halo_in, halo_ss, halo_rs, g, d).start()

    deep = 2 * levels // n_lon
    loads[0].wait()
    loads[1].wait()
    blocks = []
    for i in range(n_lon):
        g, place = i * deep // (2 * size), i * deep % (2 * size)
        source, first = (innov_ref, ivar_ref)[place // size], g * size + place % size
        blocks.append(jnp.concatenate([source[first : first + deep, p, :] for p in range(n_lat)], axis=0))
    for q, block in enumerate(swap_blocks(blocks)):
        turned[q] = block

    loads[2].wait()
    control_loads[0].wait()
    halo_pack(0)
    for load in loads[3:]:
        load.wait()
    describe(mask_ref, row_ref, col_ref, frow_ref, fcol_ref, counts_ref, meta.at[1])

    pl.semaphore_wait(barrier, n_lon - 1 + n_lat - 1)

    def first_copy(d):
        return pltpu.make_async_remote_copy(
            src_ref=turned.at[lax.rem(lon + d, n_lon)], dst_ref=land_a.at[lon],
            send_sem=a_ss.at[0], recv_sem=a_rs.at[0],
            device_id={"lon": lax.rem(lon + d, n_lon), "lat": lat},
        )

    def first_all():
        every = pl.ds(0, n_lon - 1)
        return pltpu.make_async_remote_copy(
            src_ref=turned.at[every], dst_ref=land_a.at[every],
            send_sem=a_ss.at[0], recv_sem=a_rs.at[0], device_id=sides[1],
        )

    @pl.loop(1, n_lon)
    def _(d):
        first_copy(d).start()

    halo_send(0)
    def end_copy(src, dst, send_sem, recv_sem, d):
        return pltpu.make_async_remote_copy(
            src_ref=src, dst_ref=dst, send_sem=send_sem, recv_sem=recv_sem, device_id=ends[d][0]
        )

    def at_ends(body):
        for d in range(2):
            pl.when(ends[d][1])(functools.partial(body, d))

    def meta_copy(d):
        return end_copy(meta.at[1], meta.at[2 * (1 - d)], meta_ss.at[d], meta_rs.at[1 - d], d)

    at_ends(lambda d: meta_copy(d).start())
    for load in control_loads[1:]:
        load.wait()

    @pl.loop(1, GROUPS)
    def _(g):
        halo_pack(g)
        halo_send(g)

    for d in range(2):

        @pl.when(jnp.logical_not(ends[d][1]))
        def _():
            meta[2 * d] = jnp.zeros(meta.shape[1:], F32)
            v[2 * d] = jnp.zeros(v.shape[1:], F32)
            parts_in[d] = jnp.zeros(parts_in.shape[1:], F32)

    flat = jnp.concatenate([std_ref[i : i + 1, :] for i in range(std_ref.shape[0])], axis=1)
    eye = iota((levels, levels), 0) == iota((levels, levels), 1)
    scales[...] = jnp.sum(jnp.where(eye, flat, 0.0), axis=1, keepdims=True)

    k = iota((2 * width, width), 0)
    place = jnp.where(k < width, k, jnp.where(k < width + HALF, k - (width + HALF), k - HALF))
    place = jnp.where(k < width + 2 * HALF, place, 1000.0)
    ghi, glo = split(taps(place - iota((2 * width, width), 1)))
    filt[:, 0:width] = ghi
    filt[:, width : 2 * width] = glo

    def tables(t):
        shift = jnp.asarray((t - 1) * height, jnp.int32).astype(F32)

        @pl.loop(0, chunks, unroll=4)
        def _(c):
            at = pl.ds(pl.multiple_of(c * CHUNK, CHUNK), CHUNK)
            m = meta[t, :, at]
            y = m[0:1] + shift - iota((height, CHUNK), 0)
            near, far = taps(y), taps(y + 1.0)
            weight[t, c, :, 0:CHUNK] = m[2:3] * near + m[4:5] * far
            weight[t, c, :, CHUNK : 2 * CHUNK] = m[3:4] * near + m[5:6] * far
            ytap[t, :, at] = near
            ylast[t, :, at] = taps(m[0:1] + (shift + 1.0) + 0.0 * iota((8, CHUNK), 0))
            x = iota((width, CHUNK), 0) - m[1:2]
            onehot[t, c, :, 0:CHUNK] = jnp.where(x == 0.0, 1.0, 0.0).astype(BF16)
            onehot[t, c, :, CHUNK : 2 * CHUNK] = jnp.where(x == 1.0, 1.0, 0.0).astype(BF16)
            turn = jnp.transpose(m)
            x = iota((CHUNK, width), 1) - turn[:, 1:2]
            w = jnp.concatenate(
                [
                    jnp.where(x == 0.0, turn[:, 2 + 2 * i : 3 + 2 * i], 0.0)
                    + jnp.where(x == 1.0, turn[:, 3 + 2 * i : 4 + 2 * i], 0.0)
                    for i in range(2)
                ],
                axis=1,
            )
            hi, lo = split(w)
            spreadw[t, 0, at, :] = hi
            spreadw[t, 1, at, :] = lo

    tables(1)

    land_a[pl.ds(lon, 1)] = turned[pl.ds(lon, 1)]


    first_all().wait_recv()

    for i, block in enumerate(swap_blocks([land_a[t] for t in range(n_lon)])):
        for p in range(n_lat):
            stage[p, i * deep : (i + 1) * deep] = block[p * deep : (p + 1) * deep]

    def second_copy(o, d, source, target):
        at = pl.ds(pl.multiple_of(o * 2 * size, size), 2 * size)
        return pltpu.make_async_remote_copy(
            src_ref=stage.at[source, at], dst_ref=land_b.at[target, at],
            send_sem=b_ss.at[0], recv_sem=b_rs.at[o],
            device_id={"lon": lon, "lat": source},
        )

    def second_send(o, d):
        return second_copy(o, d, lax.rem(lat + d, n_lat), lat)

    @pl.loop(0, GROUPS)
    def _(o):
        @pl.loop(1, n_lat)
        def _(d):
            second_send(o, d).start()

    land_b[pl.ds(lat, 1)] = stage[pl.ds(lat, 1)]

    at_ends(lambda d: end_copy(meta.at[1], meta.at[2 * d], meta_ss.at[d], meta_rs.at[d], d).wait_recv())

    @pl.loop(0, 2)
    def _(d):
        tables(2 * d)

    def take_observations(o):
        every, at = pl.ds(0, n_lat - 1), pl.ds(pl.multiple_of(o * 2 * size, size), 2 * size)
        pltpu.make_async_remote_copy(
            src_ref=stage.at[every, at], dst_ref=land_b.at[every, at],
            send_sem=b_ss.at[0], recv_sem=b_rs.at[o], device_id=sides[1],
        ).wait_recv()

    def smooth(x, beyond):
        hi, lo = split(jnp.concatenate([x, beyond], axis=1))
        wide = dot(hi, filt[...])
        return wide[:, :width] + wide[:, width:] + dot(lo, filt[:, 0:width])

    def part_copy(g, d):
        return end_copy(parts.at[2 * d, g], parts_in.at[1 - d, g], part_ss.at[d], part_rs.at[1 - d, g], d)

    def forward(g):
        side_wait(halo_out, halo_in, halo_ss, halo_rs, g)
        hi, lo = split(smooth(masked(g), unpack(halo_in[0, g], halo_in[1, g], rows)))
        ahl[:, 0:width] = hi
        ahl[:, width : 2 * width] = lo
        def gather(t, c):
            one = onehot[t, c]
            wide = dot(ahl[...], jnp.concatenate([one, one], axis=0))
            total = jnp.sum(wide.reshape(size, height, 2 * CHUNK) * weight[t, c][None], axis=1)
            at = pl.ds(pl.multiple_of(c * CHUNK, CHUNK), CHUNK)
            parts[t, g, :, at] = total[:, :CHUNK] + total[:, CHUNK:]

        @pl.loop(0, 3, unroll=3)
        def _(k):
            t = lax.rem(2 * k, 3)

            @pl.loop(0, chunks, unroll=4)
            def _(c):
                gather(t, c)

            @pl.when(k == 1)
            def _():
                at_ends(lambda d: part_copy(g, d).start())

    def v_copy(g, d):
        return end_copy(v.at[1, g], v.at[2 * (1 - d), g], v_ss.at[d], v_rs.at[1 - d, g], d)

    def misfit(g):
        at_ends(
            lambda d: end_copy(
                parts.at[2 * d, g], parts_in.at[d, g], part_ss.at[d], part_rs.at[d, g], d
            ).wait_recv()
        )
        scale = scales[pl.ds(pl.multiple_of(g * size, size), size), :]
        total = parts[1, g] + parts_in[0, g] + parts_in[1, g]
        take_observations(g)
        innov, ivar = (
            jnp.concatenate(
                [land_b[s, pl.ds(pl.multiple_of((2 * g + k) * size, size), size), :] for s in range(n_lat)], axis=1
            )
            for k in range(2)
        )
        v[1, g] = scale * ivar * (scale * total - innov)
        at_ends(lambda d: v_copy(g, d).start())

    def backward(g):
        at_ends(
            lambda d: end_copy(v.at[1, g], v.at[2 * d, g], v_ss.at[d], v_rs.at[d, g], d).wait_recv()
        )
        grown[...] = jnp.zeros_like(grown)

        @pl.loop(0, 3 * pairs, unroll=6)
        def _(i):
            t, c = i // pairs, i % pairs
            at = pl.ds(pl.multiple_of(c * 2 * CHUNK, 2 * CHUNK), 2 * CHUNK)
            value = v[t, g, :, at]
            b = (value[:, None, :] * ytap[t, :, at][None]).reshape(rows, 2 * CHUNK)
            last = value * ylast[t, 0:1, at]
            spare = grown.shape[0] - rows - size
            extra = jnp.concatenate([last, jnp.zeros((spare, 2 * CHUNK), F32)], axis=0) if spare else last
            hi, lo = split(jnp.concatenate([b, extra], axis=0))
            whi, wlo = spreadw[t, 0, at, :], spreadw[t, 1, at, :]
            total = dot(jnp.concatenate([hi, lo, hi], axis=1), jnp.concatenate([whi, whi, wlo], axis=0))
            grown[...] += total

        below = pltpu.roll(grown[0:rows, width : 2 * width], 1, 0)
        first = grown[rows : rows + size, width : 2 * width]
        first = jnp.broadcast_to(first[:, None, :], (size, height, width)).reshape(rows, width)
        row = lax.broadcasted_iota(jnp.int32, (size, height, width), 1).reshape(rows, width)
        x = grown[0:rows, 0:width] + jnp.where(row == 0, first, below)
        field[g] = x
        pack_sides(x, back_out, g)
        for d in range(2):
            side_copy(back_out, back_in, back_ss, back_rs, g, d).start()

    def finish(g):
        side_wait(back_out, back_in, back_ss, back_rs, g)
        x = smooth(field[g], unpack(back_in[0, g], back_in[1, g], rows))
        at = pl.ds(g * size, size)
        out_ref[at] = mask_ref[...].astype(F32)[None] * x.reshape(size, height, width)

    @pl.loop(0, GROUPS + 2)
    def _(step):
        pl.when(step < GROUPS)(lambda: forward(step))
        pl.when((step >= 1) & (step < GROUPS + 1))(lambda: misfit(step - 1))
        pl.when(step >= 2)(lambda: backward(step - 2))

    @pl.loop(0, GROUPS)
    def _(g):
        finish(g)

    def all_sent(source, sem):
        pltpu.make_async_remote_copy(
            src_ref=source, dst_ref=source, send_sem=sem, recv_sem=sem, device_id=sides[1]
        ).wait_send()

    all_sent(halo_out, halo_ss.at[0])
    all_sent(back_out, back_ss.at[0])
    all_sent(turned.at[pl.ds(0, n_lon - 1)], a_ss.at[0])
    all_sent(stage.at[pl.ds(0, n_lat - 1)], b_ss.at[0])

    def ends_sent(d):
        all_sent(parts.at[2 * d], part_ss.at[d])
        all_sent(v.at[1], v_ss.at[d])
        meta_copy(d).wait_send()

    at_ends(ends_sent)


def shards(n_lon, n_lat, control, land_mask, std_dev, innovation, inverse_var, *slots_of):
    levels = control.shape[0] * control.shape[1]
    height, width = control.shape[2:]
    slots = slots_of[0].shape[0] * slots_of[0].shape[1]
    chunks = slots // CHUNK
    size = levels // GROUPS
    rows = size * height
    packed = packing(rows)[0]
    grown = -(-(rows + size) // 16) * 16
    deep = 2 * levels // n_lon
    dma = pltpu.SemaphoreType.DMA
    group, both, one = dma((2, GROUPS)), dma((2,)), dma((1,))
    sides = pltpu.VMEM((2, GROUPS, packed, width), F32)

    inputs = [
        control.reshape(levels, height, width), land_mask, std_dev, innovation, inverse_var, *slots_of,
    ]
    gradient = pl.pallas_call(
        functools.partial(kernel, n_lon, n_lat),
        out_shape=pltpu.VMEM((levels, height, width), F32),
        in_specs=[HBM] * 10,
        out_specs=VMEM,
        scratch_shapes=[pltpu.VMEM(x.shape, x.dtype) for x in inputs] + [
            pltpu.VMEM((2 * width, 2 * width), BF16),
            sides, sides, sides, sides,
            pltpu.VMEM((rows, 2 * width), BF16),
            pltpu.VMEM((grown, 2 * width), F32),
            pltpu.VMEM((GROUPS, rows, width), F32),
            pltpu.VMEM((3, 8, slots), F32),
            pltpu.VMEM((3, chunks, width, 2 * CHUNK), BF16),
            pltpu.VMEM((3, chunks, height, 2 * CHUNK), F32),
            pltpu.VMEM((3, height, slots), F32),
            pltpu.VMEM((3, 8, slots), F32),
            pltpu.VMEM((3, 2, slots, 2 * width), BF16),
            pltpu.VMEM((3, GROUPS, size, slots), F32),
            pltpu.VMEM((2, GROUPS, size, slots), F32),
            pltpu.VMEM((3, GROUPS, size, slots), F32),
            pltpu.VMEM((n_lon, n_lat * deep, width), F32),
            pltpu.VMEM((n_lon, n_lat * deep, width), F32),
            pltpu.VMEM((n_lat, 2 * levels, width), F32),
            pltpu.VMEM((n_lat, 2 * levels, width), F32),
            pltpu.VMEM((levels, 1), F32),
            one, group, one, group, both, both, both, group, both, group, one, one, one, dma((GROUPS,)),
            dma((9,)), dma((GROUPS,)),
        ],
        compiler_params=pltpu.CompilerParams(
            vmem_limit_bytes=56 << 20, collective_id=0, has_side_effects=True
        ),
        name="gradient",
    )(*inputs)
    return control + gradient.reshape(control.shape)


def solution(mesh):
    tile = P("lat", "lon")
    in_specs = (
        P(None, None, "lat", "lon"), tile, P(),
        P(None, "lat", "lon"), P(None, "lat", "lon"),
        tile, tile, tile, tile, tile,
    )
    body = functools.partial(shards, mesh.shape["lon"], mesh.shape["lat"])
    return jax.shard_map(
        body, mesh=mesh, in_specs=in_specs,
        out_specs=P(None, None, "lat", "lon"), check_vma=False,
    )
```

```python
import functools

import jax
import jax.numpy as jnp
import numpy as np
from jax import lax
from jax.experimental import pallas as pl
from jax.experimental.pallas import tpu as pltpu
from jax.sharding import PartitionSpec as P

HALF = 50
SPREAD = HALF / 2.0
_TAPS = np.exp(-0.5 * (np.arange(-HALF, HALF + 1) / SPREAD) ** 2)
NORM = float(1.0 / np.sqrt(np.sum(_TAPS * _TAPS)))
CHUNK = 128
GROUPS = 4
PIECE = HALF // 2
VMEM = pl.BlockSpec(memory_space=pltpu.VMEM)
HBM = pl.BlockSpec(memory_space=pltpu.HBM)
F32, BF16 = jnp.float32, jnp.bfloat16


def split(x):
    hi = x.astype(BF16)
    return hi, (x - hi.astype(F32)).astype(BF16)


def taps(distance):
    values = jnp.exp(distance * distance * (-0.5 / (SPREAD * SPREAD))) * NORM
    return jnp.where(jnp.abs(distance) < HALF + 0.5, values, 0.0)


def iota(shape, dim):
    return lax.broadcasted_iota(jnp.int32, shape, dim).astype(F32)


def dot(a, b):
    return jnp.dot(a, b, preferred_element_type=F32)


def roll(x, shift):
    shift = shift % x.shape[1]
    return pltpu.roll(x, shift, 1) if shift else x


def packing(rows):
    per = 128 // PIECE
    packed = -(-2 * rows // (8 * per)) * 8
    segments, at = [], 0
    while at < 2 * rows:
        half, row = at // rows, at % rows
        slot, place = at // packed, at % packed
        count = min(rows - row, packed - place)
        segments.append((half, row, count, slot, place))
        at += count
    return packed, segments


def pack(x, first):
    rows, width = x.shape
    packed, segments = packing(rows)
    lane = lax.broadcasted_iota(jnp.int32, (packed, width), 1)
    result = None
    for slot in range(segments[-1][3] + 1):
        mine = [s for s in segments if s[3] == slot]
        pieces = [
            roll(x[row : row + count], slot * PIECE - (first + half * PIECE))
            for half, row, count, _, _ in mine
        ]
        lacking = packed - sum(s[2] for s in mine)
        if lacking:
            pieces.append(x[:lacking])
        piece = jnp.concatenate(pieces, axis=0) if len(pieces) > 1 else pieces[0]
        result = piece if result is None else jnp.where(lane >= slot * PIECE, piece, result)
    return result


def unpack(left, right, rows):
    _, segments = packing(rows)
    lane = lax.broadcasted_iota(jnp.int32, (rows, left.shape[1]), 1)
    result = None
    for k, source in enumerate((left, right)):
        for half in range(2):
            target = k * HALF + half * PIECE
            pieces = [
                roll(source[place : place + count], target - slot * PIECE)
                for h, _, count, slot, place in segments
                if h == half
            ]
            piece = jnp.concatenate(pieces, axis=0)
            result = piece if result is None else jnp.where(lane >= target, piece, result)
    return result


def swap_blocks(blocks):
    count = len(blocks)
    width = blocks[0].shape[1] // count
    group = lax.broadcasted_iota(jnp.int32, blocks[0].shape, 1) // width
    bit = 1
    while bit < count:
        low = (group & bit) == 0
        fresh = []
        for k in range(count):
            other = blocks[k ^ bit]
            if k & bit == 0:
                fresh.append(jnp.where(low, blocks[k], roll(other, width * bit)))
            else:
                fresh.append(jnp.where(low, roll(other, -width * bit), blocks[k]))
        blocks = fresh
        bit *= 2
    return blocks


def describe(mask_ref, row_ref, col_ref, frow_ref, fcol_ref, counts_ref, out_ref):
    mask = mask_ref[...].astype(BF16)
    height, width = mask.shape
    holders, lanes = row_ref.shape
    tiles = counts_ref.shape[1]
    cap = lanes // tiles
    tile = lax.broadcasted_iota(jnp.int32, (tiles, lanes), 0)
    lane = lax.broadcasted_iota(jnp.int32, (tiles, lanes), 1)
    inside = (lane >= tile * cap) & (lane < tile * cap + cap)
    repeat = jnp.where(inside, 1.0, 0.0).astype(BF16)
    first = jnp.sum(jnp.where(inside, tile * cap, 0).astype(F32), axis=0, keepdims=True)
    number = iota((1, lanes), 1) - first
    limits = dot(counts_ref[...].astype(F32).astype(BF16), repeat)
    for s in range(holders):
        row = row_ref[pl.ds(s, 1), :].astype(F32)
        col = col_ref[pl.ds(s, 1), :].astype(F32)
        a = frow_ref[pl.ds(s, 1), :]
        b = fcol_ref[pl.ds(s, 1), :]
        x = iota((width, lanes), 0) - col
        both = jnp.concatenate(
            [jnp.where(x == 0.0, 1.0, 0.0).astype(BF16), jnp.where(x == 1.0, 1.0, 0.0).astype(BF16)], axis=1
        )
        found = dot(mask, both)
        left, right = found[:, :lanes], found[:, lanes:]
        y = iota((height, lanes), 0) - row
        m00 = jnp.sum(jnp.where(y == 0.0, left, 0.0), axis=0, keepdims=True)
        m01 = jnp.sum(jnp.where(y == 0.0, right, 0.0), axis=0, keepdims=True)
        m10 = jnp.sum(jnp.where(y == 1.0, left, 0.0), axis=0, keepdims=True)
        m11 = jnp.sum(jnp.where(y == 1.0, right, 0.0), axis=0, keepdims=True)
        live = jnp.where(number < limits[s : s + 1], 1.0, 0.0)
        at = pl.ds(s * lanes, lanes)
        out_ref[0:1, at] = row
        out_ref[1:2, at] = col
        out_ref[2:3, at] = (1.0 - a) * (1.0 - b) * m00 * live
        out_ref[3:4, at] = (1.0 - a) * b * m01 * live
        out_ref[4:5, at] = a * (1.0 - b) * m10 * live
        out_ref[5:6, at] = a * b * m11 * live
        out_ref[6:7, at] = live
        out_ref[7:8, at] = live


def kernel(
    n_lon, n_lat,
    control_far, mask_far, std_far, innov_far, ivar_far, row_far, col_far, frow_far, fcol_far, counts_far,
    out_ref,
    control_ref, mask_ref, std_ref, innov_ref, ivar_ref, row_ref, col_ref, frow_ref, fcol_ref, counts_ref,
    filt, halo_out, halo_in, back_out, back_in, ahl, grown, field,
    meta, onehot, weight, ytap, ylast, spreadw,
    parts, parts_in, v,
    turned, land_a, stage, land_b, scales,
    halo_ss, halo_rs, back_ss, back_rs, meta_ss, meta_rs, part_ss, part_rs, v_ss, v_rs,
    a_ss, a_rs, b_ss, b_rs, load_sem, control_sem,
):
    levels, height, width = control_ref.shape
    slots = meta.shape[2]
    chunks, pairs = slots // CHUNK, slots // (2 * CHUNK)
    size = levels // GROUPS
    rows = size * height
    lon, lat = lax.axis_index("lon"), lax.axis_index("lat")
    sides = [{"lon": lax.rem(lon + n_lon - 1, n_lon), "lat": lat}, {"lon": lax.rem(lon + 1, n_lon), "lat": lat}]
    ends = [({"lon": lon, "lat": lat - 1}, lat > 0), ({"lon": lon, "lat": lat + 1}, lat < n_lat - 1)]

    barrier = pltpu.get_barrier_semaphore()

    @pl.loop(1, n_lon, unroll=min(7, n_lon - 1))
    def _(d):
        pl.semaphore_signal(barrier, inc=1, device_id={"lon": lax.rem(lon + d, n_lon), "lat": lat})

    @pl.loop(1, n_lat, unroll=min(3, n_lat - 1))
    def _(d):
        pl.semaphore_signal(barrier, inc=1, device_id={"lon": lon, "lat": lax.rem(lat + d, n_lat)})

    far = [innov_far, ivar_far, mask_far, row_far, col_far, frow_far, fcol_far, counts_far, std_far]
    near = [innov_ref, ivar_ref, mask_ref, row_ref, col_ref, frow_ref, fcol_ref, counts_ref, std_ref]
    loads = [pltpu.make_async_copy(a, b, load_sem.at[i]) for i, (a, b) in enumerate(zip(far, near))]
    at_group = [pl.ds(g * size, size) for g in range(GROUPS)]
    control_loads = [
        pltpu.make_async_copy(control_far.at[at], control_ref.at[at], control_sem.at[g])
        for g, at in enumerate(at_group)
    ]
    for load in loads[:3] + control_loads + loads[3:]:
        load.start()

    def masked(g):
        part = control_ref[pl.ds(g * size, size)] * mask_ref[...].astype(F32)[None]
        return part.reshape(rows, width)

    def side_copy(out, landed, ss, rs, g, d):
        return pltpu.make_async_remote_copy(
            src_ref=out.at[d, g], dst_ref=landed.at[1 - d, g],
            send_sem=ss.at[0], recv_sem=rs.at[1 - d, g], device_id=sides[d],
        )

    def side_wait(out, landed, ss, rs, g):
        for d in range(2):
            pltpu.make_async_remote_copy(
                src_ref=out.at[d, g], dst_ref=landed.at[d, g],
                send_sem=ss.at[0], recv_sem=rs.at[d, g], device_id=sides[d],
            ).wait_recv()

    def pack_sides(x, out, g):
        out[0, g] = pack(x, 0)
        out[1, g] = pack(x, width - HALF)

    def halo_pack(g):
        pack_sides(masked(g), halo_out, g)

    def side_send(out, landed, ss, rs, g):
        for k in range(2):
            d = lax.rem(lon + k, 2)
            pltpu.make_async_remote_copy(
                src_ref=out.at[d, g], dst_ref=landed.at[1 - d, g], send_sem=ss.at[0], recv_sem=rs.at[1 - d, g],
                device_id={"lon": lax.rem(lon + n_lon - 1 + 2 * d, n_lon), "lat": lat},
            ).start()

    def halo_send(g):
        side_send(halo_out, halo_in, halo_ss, halo_rs, g)

    deep = 2 * levels // n_lon
    loads[0].wait()
    loads[1].wait()
    blocks = []
    for i in range(n_lon):
        g, place = i * deep // (2 * size), i * deep % (2 * size)
        source, first = (innov_ref, ivar_ref)[place // size], g * size + place % size
        blocks.append(jnp.concatenate([source[first : first + deep, p, :] for p in range(n_lat)], axis=0))
    for q, block in enumerate(swap_blocks(blocks)):
        turned[q] = block

    loads[2].wait()
    control_loads[0].wait()
    halo_pack(0)
    for load in loads[3:]:
        load.wait()
    describe(mask_ref, row_ref, col_ref, frow_ref, fcol_ref, counts_ref, meta.at[1])

    pl.semaphore_wait(barrier, n_lon - 1 + n_lat - 1)

    def first_copy(d):
        return pltpu.make_async_remote_copy(
            src_ref=turned.at[lax.rem(lon + d, n_lon)], dst_ref=land_a.at[lon],
            send_sem=a_ss.at[0], recv_sem=a_rs.at[0],
            device_id={"lon": lax.rem(lon + d, n_lon), "lat": lat},
        )

    def first_all():
        every = pl.ds(0, n_lon - 1)
        return pltpu.make_async_remote_copy(
            src_ref=turned.at[every], dst_ref=land_a.at[every],
            send_sem=a_ss.at[0], recv_sem=a_rs.at[0], device_id=sides[1],
        )

    @pl.loop(1, n_lon, unroll=min(7, n_lon - 1))
    def _(d):
        first_copy(d).start()

    halo_send(0)
    def end_copy(src, dst, send_sem, recv_sem, d):
        return pltpu.make_async_remote_copy(
            src_ref=src, dst_ref=dst, send_sem=send_sem, recv_sem=recv_sem, device_id=ends[d][0]
        )

    def at_ends(body):
        for d in range(2):
            pl.when(ends[d][1])(functools.partial(body, d))

    def meta_copy(d):
        return end_copy(meta.at[1], meta.at[2 * (1 - d)], meta_ss.at[d], meta_rs.at[1 - d], d)

    at_ends(lambda d: meta_copy(d).start())
    for load in control_loads[1:]:
        load.wait()

    @pl.loop(1, GROUPS)
    def _(g):
        halo_pack(g)
        halo_send(g)

    for d in range(2):

        @pl.when(jnp.logical_not(ends[d][1]))
        def _():
            meta[2 * d] = jnp.zeros(meta.shape[1:], F32)
            v[2 * d] = jnp.zeros(v.shape[1:], F32)
            parts_in[d] = jnp.zeros(parts_in.shape[1:], F32)

    flat = jnp.concatenate([std_ref[i : i + 1, :] for i in range(std_ref.shape[0])], axis=1)
    eye = iota((levels, levels), 0) == iota((levels, levels), 1)
    scales[...] = jnp.sum(jnp.where(eye, flat, 0.0), axis=1, keepdims=True)

    k = iota((2 * width, width), 0)
    place = jnp.where(k < width, k, jnp.where(k < width + HALF, k - (width + HALF), k - HALF))
    place = jnp.where(k < width + 2 * HALF, place, 1000.0)
    ghi, glo = split(taps(place - iota((2 * width, width), 1)))
    filt[:, 0:width] = ghi
    filt[:, width : 2 * width] = glo

    def tables(t):
        shift = jnp.asarray((t - 1) * height, jnp.int32).astype(F32)

        @pl.loop(0, chunks, unroll=4)
        def _(c):
            at = pl.ds(pl.multiple_of(c * CHUNK, CHUNK), CHUNK)
            m = meta[t, :, at]
            y = m[0:1] + shift - iota((height, CHUNK), 0)
            near, far = taps(y), taps(y + 1.0)
            weight[t, c, :, 0:CHUNK] = m[2:3] * near + m[4:5] * far
            weight[t, c, :, CHUNK : 2 * CHUNK] = m[3:4] * near + m[5:6] * far
            ytap[t, :, at] = near
            ylast[t, :, at] = taps(m[0:1] + (shift + 1.0) + 0.0 * iota((8, CHUNK), 0))
            x = iota((width, CHUNK), 0) - m[1:2]
            onehot[t, c, :, 0:CHUNK] = jnp.where(x == 0.0, 1.0, 0.0).astype(BF16)
            onehot[t, c, :, CHUNK : 2 * CHUNK] = jnp.where(x == 1.0, 1.0, 0.0).astype(BF16)
            turn = jnp.transpose(m)
            x = iota((CHUNK, width), 1) - turn[:, 1:2]
            w = jnp.concatenate(
                [
                    jnp.where(x == 0.0, turn[:, 2 + 2 * i : 3 + 2 * i], 0.0)
                    + jnp.where(x == 1.0, turn[:, 3 + 2 * i : 4 + 2 * i], 0.0)
                    for i in range(2)
                ],
                axis=1,
            )
            hi, lo = split(w)
            spreadw[t, 0, at, :] = hi
            spreadw[t, 1, at, :] = lo

    tables(1)

    land_a[pl.ds(lon, 1)] = turned[pl.ds(lon, 1)]


    first_all().wait_recv()

    for i, block in enumerate(swap_blocks([land_a[t] for t in range(n_lon)])):
        for p in range(n_lat):
            stage[p, i * deep : (i + 1) * deep] = block[p * deep : (p + 1) * deep]

    def second_copy(o, d, source, target):
        at = pl.ds(pl.multiple_of(o * 2 * size, size), 2 * size)
        return pltpu.make_async_remote_copy(
            src_ref=stage.at[source, at], dst_ref=land_b.at[target, at],
            send_sem=b_ss.at[0], recv_sem=b_rs.at[o],
            device_id={"lon": lon, "lat": source},
        )

    def second_send(o, d):
        return second_copy(o, d, lax.rem(lat + d, n_lat), lat)

    @pl.loop(0, GROUPS)
    def _(o):
        @pl.loop(1, n_lat, unroll=min(3, n_lat - 1))
        def _(d):
            second_send(o, d).start()

    land_b[pl.ds(lat, 1)] = stage[pl.ds(lat, 1)]

    at_ends(lambda d: end_copy(meta.at[1], meta.at[2 * d], meta_ss.at[d], meta_rs.at[d], d).wait_recv())

    @pl.loop(0, 2)
    def _(d):
        tables(2 * d)

    def take_observations(o):
        every, at = pl.ds(0, n_lat - 1), pl.ds(pl.multiple_of(o * 2 * size, size), 2 * size)
        pltpu.make_async_remote_copy(
            src_ref=stage.at[every, at], dst_ref=land_b.at[every, at],
            send_sem=b_ss.at[0], recv_sem=b_rs.at[o], device_id=sides[1],
        ).wait_recv()

    def smooth(x, beyond):
        hi, lo = split(jnp.concatenate([x, beyond], axis=1))
        wide = dot(hi, filt[...])
        return wide[:, :width] + wide[:, width:] + dot(lo, filt[:, 0:width])

    def part_copy(g, d):
        return end_copy(parts.at[2 * d, g], parts_in.at[1 - d, g], part_ss.at[d], part_rs.at[1 - d, g], d)

    def forward(g):
        side_wait(halo_out, halo_in, halo_ss, halo_rs, g)
        hi, lo = split(smooth(masked(g), unpack(halo_in[0, g], halo_in[1, g], rows)))
        ahl[:, 0:width] = hi
        ahl[:, width : 2 * width] = lo
        def gather(t, c):
            one = onehot[t, c]
            wide = dot(ahl[...], jnp.concatenate([one, one], axis=0))
            total = jnp.sum(wide.reshape(size, height, 2 * CHUNK) * weight[t, c][None], axis=1)
            at = pl.ds(pl.multiple_of(c * CHUNK, CHUNK), CHUNK)
            parts[t, g, :, at] = total[:, :CHUNK] + total[:, CHUNK:]

        @pl.loop(0, 3, unroll=3)
        def _(k):
            t = lax.rem(2 * k, 3)

            @pl.loop(0, chunks, unroll=4)
            def _(c):
                gather(t, c)

            @pl.when(k == 1)
            def _():
                at_ends(lambda d: part_copy(g, d).start())

    def v_copy(g, d):
        return end_copy(v.at[1, g], v.at[2 * (1 - d), g], v_ss.at[d], v_rs.at[1 - d, g], d)

    def misfit(g):
        at_ends(
            lambda d: end_copy(
                parts.at[2 * d, g], parts_in.at[d, g], part_ss.at[d], part_rs.at[d, g], d
            ).wait_recv()
        )
        scale = scales[pl.ds(pl.multiple_of(g * size, size), size), :]
        total = parts[1, g] + parts_in[0, g] + parts_in[1, g]
        take_observations(g)
        innov, ivar = (
            jnp.concatenate(
                [land_b[s, pl.ds(pl.multiple_of((2 * g + k) * size, size), size), :] for s in range(n_lat)], axis=1
            )
            for k in range(2)
        )
        v[1, g] = scale * ivar * (scale * total - innov)
        at_ends(lambda d: v_copy(g, d).start())

    def backward(g):
        at_ends(
            lambda d: end_copy(v.at[1, g], v.at[2 * d, g], v_ss.at[d], v_rs.at[d, g], d).wait_recv()
        )
        grown[...] = jnp.zeros_like(grown)

        @pl.loop(0, 3 * pairs, unroll=6)
        def _(i):
            t, c = i // pairs, i % pairs
            at = pl.ds(pl.multiple_of(c * 2 * CHUNK, 2 * CHUNK), 2 * CHUNK)
            value = v[t, g, :, at]
            b = (value[:, None, :] * ytap[t, :, at][None]).reshape(rows, 2 * CHUNK)
            last = value * ylast[t, 0:1, at]
            spare = grown.shape[0] - rows - size
            extra = jnp.concatenate([last, jnp.zeros((spare, 2 * CHUNK), F32)], axis=0) if spare else last
            hi, lo = split(jnp.concatenate([b, extra], axis=0))
            whi, wlo = spreadw[t, 0, at, :], spreadw[t, 1, at, :]
            total = dot(jnp.concatenate([hi, lo, hi], axis=1), jnp.concatenate([whi, whi, wlo], axis=0))
            grown[...] += total

        below = pltpu.roll(grown[0:rows, width : 2 * width], 1, 0)
        first = grown[rows : rows + size, width : 2 * width]
        first = jnp.broadcast_to(first[:, None, :], (size, height, width)).reshape(rows, width)
        row = lax.broadcasted_iota(jnp.int32, (size, height, width), 1).reshape(rows, width)
        x = grown[0:rows, 0:width] + jnp.where(row == 0, first, below)
        field[g] = x
        pack_sides(x, back_out, g)
        side_send(back_out, back_in, back_ss, back_rs, g)

    def finish(g):
        side_wait(back_out, back_in, back_ss, back_rs, g)
        x = smooth(field[g], unpack(back_in[0, g], back_in[1, g], rows))
        at = pl.ds(g * size, size)
        out_ref[at] = control_ref[at] + mask_ref[...].astype(F32)[None] * x.reshape(size, height, width)

    @pl.loop(0, GROUPS + 2)
    def _(step):
        pl.when(step < GROUPS)(lambda: forward(step))
        pl.when((step >= 1) & (step < GROUPS + 1))(lambda: misfit(step - 1))
        pl.when(step >= 2)(lambda: backward(step - 2))

    @pl.loop(0, GROUPS)
    def _(g):
        finish(g)

    def all_sent(source, sem):
        pltpu.make_async_remote_copy(
            src_ref=source, dst_ref=source, send_sem=sem, recv_sem=sem, device_id=sides[1]
        ).wait_send()

    all_sent(halo_out, halo_ss.at[0])
    all_sent(back_out, back_ss.at[0])
    all_sent(turned.at[pl.ds(0, n_lon - 1)], a_ss.at[0])
    all_sent(stage.at[pl.ds(0, n_lat - 1)], b_ss.at[0])

    def ends_sent(d):
        all_sent(parts.at[2 * d], part_ss.at[d])
        all_sent(v.at[1], v_ss.at[d])
        meta_copy(d).wait_send()

    at_ends(ends_sent)


def shards(n_lon, n_lat, control, land_mask, std_dev, innovation, inverse_var, *slots_of):
    levels = control.shape[0] * control.shape[1]
    height, width = control.shape[2:]
    slots = slots_of[0].shape[0] * slots_of[0].shape[1]
    chunks = slots // CHUNK
    size = levels // GROUPS
    rows = size * height
    packed = packing(rows)[0]
    grown = -(-(rows + size) // 16) * 16
    deep = 2 * levels // n_lon
    dma = pltpu.SemaphoreType.DMA
    group, both, one = dma((2, GROUPS)), dma((2,)), dma((1,))
    sides = pltpu.VMEM((2, GROUPS, packed, width), F32)

    inputs = [
        control.reshape(levels, height, width), land_mask, std_dev, innovation, inverse_var, *slots_of,
    ]
    gradient = pl.pallas_call(
        functools.partial(kernel, n_lon, n_lat),
        out_shape=pltpu.VMEM((levels, height, width), F32),
        in_specs=[HBM] * 10,
        out_specs=VMEM,
        scratch_shapes=[pltpu.VMEM(x.shape, x.dtype) for x in inputs] + [
            pltpu.VMEM((2 * width, 2 * width), BF16),
            sides, sides, sides, sides,
            pltpu.VMEM((rows, 2 * width), BF16),
            pltpu.VMEM((grown, 2 * width), F32),
            pltpu.VMEM((GROUPS, rows, width), F32),
            pltpu.VMEM((3, 8, slots), F32),
            pltpu.VMEM((3, chunks, width, 2 * CHUNK), BF16),
            pltpu.VMEM((3, chunks, height, 2 * CHUNK), F32),
            pltpu.VMEM((3, height, slots), F32),
            pltpu.VMEM((3, 8, slots), F32),
            pltpu.VMEM((3, 2, slots, 2 * width), BF16),
            pltpu.VMEM((3, GROUPS, size, slots), F32),
            pltpu.VMEM((2, GROUPS, size, slots), F32),
            pltpu.VMEM((3, GROUPS, size, slots), F32),
            pltpu.VMEM((n_lon, n_lat * deep, width), F32),
            pltpu.VMEM((n_lon, n_lat * deep, width), F32),
            pltpu.VMEM((n_lat, 2 * levels, width), F32),
            pltpu.VMEM((n_lat, 2 * levels, width), F32),
            pltpu.VMEM((levels, 1), F32),
            one, group, one, group, both, both, both, group, both, group, one, one, one, dma((GROUPS,)),
            dma((9,)), dma((GROUPS,)),
        ],
        compiler_params=pltpu.CompilerParams(
            vmem_limit_bytes=56 << 20, collective_id=0, has_side_effects=True
        ),
        name="gradient",
    )(*inputs)
    return gradient.reshape(control.shape)


def solution(mesh):
    tile = P("lat", "lon")
    in_specs = (
        P(None, None, "lat", "lon"), tile, P(),
        P(None, "lat", "lon"), P(None, "lat", "lon"),
        tile, tile, tile, tile, tile,
    )
    body = functools.partial(shards, mesh.shape["lon"], mesh.shape["lat"])
    return jax.shard_map(
        body, mesh=mesh, in_specs=in_specs,
        out_specs=P(None, None, "lat", "lon"), check_vma=False,
    )
```
